128 devices in a mesh: blk: 16 (over y, x_hi, core), head: 8 (over x_lo, z).
Axes of the slice: x: 4 (x_hi: 2, x_lo: 2; x = x_hi * 2 + x_lo), y: 4, z: 4, core: 2. Of those that a mesh axis runs over, the one named last changes fastest.
Arguments:
- queries: bfloat16 [1, 16384, 2048], P(None, ('blk', 'head')), may hold values from -5 to 5
- keys: bfloat16 [1, 16384, 512], P(None, ('blk', 'head')), may hold values from -5 to 5
- values: bfloat16 [1, 16384, 512], P(None, ('blk', 'head')), may hold values from -6 to 6
- upstream: bfloat16 [1, 16384, 2048], P(None, ('blk', 'head')), may hold values from -6 to 6
- tile_mask: int32 [1, 128, 128], replicated, may hold values from 0 to 1, as said below
- tile_order: int32 [1, 128], replicated, may hold values from 0 to 127, as said below
Outputs:
- attended: bfloat16 [1, 16384, 2048], P(None, ('blk', 'head'))
- grad_queries: bfloat16 [1, 16384, 2048], P(None, ('blk', 'head'))
- grad_keys: bfloat16 [1, 16384, 512], P(None, ('blk', 'head'))
- grad_values: bfloat16 [1, 16384, 512], P(None, ('blk', 'head'))
The draws below stay inside these ranges and needn't reach their ends.
Inputs may be any that keep to these rules, and one draw needn't show every extreme that they name: With b(i) = i // 8 the position block of tile i: tile_mask[s, i, j] is 1 where i == j or j == 0, 0 where j > i, and 0 where b(i) - b(j) >= 3 and b(j) > 0. Whole position blocks of 8 tiles keep their inner order: tile_order[s, k * 8 + t] = p[k] * 8 + t for a permutation p of the position blocks.
All inputs are finite; a program needn't handle non-finite values.
Results may differ from the reference program's by a relative error of at most 0.012.
The reference program's roundings to bfloat16 on the way (of `probs_low` and `grad_scores`) count: a program that leaves them out, or rounds other values in their place, can miss the bound.
Values may be sent and summed in bfloat16 or wider, within the bound.
No kernel may reach another device: no remote copies, remote signals or barrier semaphores. Data moves between devices by JAX's collectives and lax.ppermute only.
A program may use at most 128 MiB of HBM per device.

```python
import math
import jax
import jax.numpy as jnp
from jax import lax

HD = 128
QH = 16
KVH = 4
TILE = 128
SEQS = 1
SEQ = 16384
NTILE = 128
RB = 1024


def draw_keys(key, part):
    key = jax.random.fold_in(key, 11)
    bulk = jnp.clip(jax.random.normal(key, (SEQS, SEQ, KVH * HD), jnp.float32) * 1.6, -5.0, 5.0)
    return bulk.astype(jnp.bfloat16)


def draw_queries(key, part):
    key = jax.random.fold_in(key, 12)
    bulk = jnp.clip(jax.random.normal(key, (SEQS, SEQ, QH * HD), jnp.float32) * 1.6, -5.0, 5.0)
    return bulk.astype(jnp.bfloat16)


def draw_tile_mask(key, part):
    key = jax.random.fold_in(key, 13)
    per_block = RB // TILE
    row_tiles = jnp.arange(NTILE, dtype=jnp.int32)[:, None]
    col_tiles = jnp.arange(NTILE, dtype=jnp.int32)[None, :]
    row_block = row_tiles // per_block
    col_block = col_tiles // per_block
    coins = jax.random.randint(key, (SEQS, NTILE, NTILE), 0, 5)
    earlier = col_tiles < row_tiles
    window = earlier & (row_block - col_block < 3) & (coins < 3)
    sink = earlier & (col_block == 0) & (coins < 2)
    fixed = (row_tiles == col_tiles) | (col_tiles == 0)
    return (fixed | window | sink).astype(jnp.int32)


def draw_tile_order(key, part):
    key = jax.random.fold_in(key, 14)
    per_block = RB // TILE
    block_total = NTILE // per_block
    inner = jnp.arange(per_block, dtype=jnp.int32)
    rows = []
    for seq_index in range(SEQS):
        shuffled = jax.random.permutation(jax.random.fold_in(key, seq_index), block_total).astype(jnp.int32)
        rows.append((shuffled[:, None] * per_block + inner[None, :]).reshape(NTILE))
    return jnp.stack(rows)


def block_levels(stream_key, extent, pieces, low, high):
    def one(dim, blocks):
        steps = jax.random.uniform(jax.random.fold_in(jax.random.fold_in(stream_key, 6), dim), (blocks,), jnp.float32, low / len(pieces), high / len(pieces))
        return jnp.repeat(jnp.exp(steps), extent[dim] // blocks).reshape((-1,) + (1,) * (len(extent) - dim - 1))

    gain = one(*pieces[0])
    for cut in pieces[1:]:
        gain = gain * one(*cut)
    return gain


def noise(rng, shape, scale, bound, shards=(), kind=jnp.bfloat16):
    values = scale * jax.random.normal(rng, shape, jnp.float32)
    if shards:
        values = values * block_levels(rng, shape, shards, -0.22, 0.18)
    return jnp.clip(values, -bound, bound).astype(kind)


def setup_inputs(seed: int = 0) -> dict:
    arg_keys = jax.random.split(jax.random.key(seed), 7)
    return {
        "queries": draw_queries(jax.random.fold_in(arg_keys[6], 71), 0),
        "keys": draw_keys(jax.random.fold_in(arg_keys[6], 71), 0),
        "values": noise(arg_keys[2], (SEQS, SEQ, KVH * HD), 1.0, 6.0, ((1, 128),)),
        "upstream": noise(arg_keys[3], (SEQS, SEQ, QH * HD), 1.0, 6.0, ((1, 128),)),
        "tile_mask": draw_tile_mask(jax.random.fold_in(arg_keys[6], 71), 0),
        "tile_order": draw_tile_order(jax.random.fold_in(arg_keys[6], 71), 0),
    }


def visibility(order, tiles):
    row_ids = jnp.arange(SEQ, dtype=jnp.int32)
    place_tile = jnp.repeat(order, TILE)
    place = place_tile * TILE + row_ids % TILE
    live = tiles[place_tile[:, None], place_tile[None, :]] == 1
    return live & (place[None, :] <= place[:, None])

def one_head(query, key_rows, value_rows, cotangent, allowed):
    inv_root = 1.0 / math.sqrt(HD)
    scores = jnp.dot(query, key_rows.T, preferred_element_type=jnp.float32) * inv_root
    masked = jnp.where(allowed, scores, -jnp.inf)
    row_top = lax.optimization_barrier(jnp.max(masked, axis=1, keepdims=True))
    log_total = row_top + jnp.log(lax.optimization_barrier(jnp.sum(jnp.exp(masked - row_top), axis=1, keepdims=True)))
    probs = jnp.exp(masked - log_total)
    probs_low = probs.astype(jnp.bfloat16)
    attended = jnp.dot(probs_low, value_rows, preferred_element_type=jnp.float32).astype(jnp.bfloat16)
    delta = lax.optimization_barrier(jnp.sum(cotangent.astype(jnp.float32) * attended.astype(jnp.float32), axis=1, keepdims=True))
    grad_probs = jnp.dot(cotangent, value_rows.T, preferred_element_type=jnp.float32)
    grad_scores = (probs * (grad_probs - delta)).astype(jnp.bfloat16)
    grad_query = (jnp.dot(grad_scores, key_rows, preferred_element_type=jnp.float32) * inv_root).astype(jnp.bfloat16)
    grad_key = jnp.dot(grad_scores.T, query, preferred_element_type=jnp.float32) * inv_root
    grad_value = jnp.dot(probs_low.T, cotangent, preferred_element_type=jnp.float32)
    return (attended, grad_query, grad_key, grad_value)

def reference(queries, keys, values, upstream, tile_mask, tile_order):
    group = QH // KVH
    outs_all, gq_all, gk_all, gv_all = ([], [], [], [])
    for seq_index in range(SEQS):
        allowed = visibility(tile_order[seq_index], tile_mask[seq_index])
        q_heads = queries[seq_index].reshape(SEQ, QH, HD).transpose(1, 0, 2)
        d_heads = upstream[seq_index].reshape(SEQ, QH, HD).transpose(1, 0, 2)
        k_heads = jnp.repeat(keys[seq_index].reshape(SEQ, KVH, HD).transpose(1, 0, 2), group, axis=0)
        v_heads = jnp.repeat(values[seq_index].reshape(SEQ, KVH, HD).transpose(1, 0, 2), group, axis=0)

        def run_head(items):
            return one_head(items[0], items[1], items[2], items[3], allowed)
        attended, grad_query, grad_key, grad_value = lax.map(run_head, (q_heads, k_heads, v_heads, d_heads))
        grad_key = grad_key.reshape(KVH, group, SEQ, HD).sum(axis=1)
        grad_value = grad_value.reshape(KVH, group, SEQ, HD).sum(axis=1)
        outs_all.append(attended.transpose(1, 0, 2).reshape(SEQ, QH * HD))
        gq_all.append(grad_query.transpose(1, 0, 2).reshape(SEQ, QH * HD))
        gk_all.append(grad_key.transpose(1, 0, 2).reshape(SEQ, KVH * HD).astype(jnp.bfloat16))
        gv_all.append(grad_value.transpose(1, 0, 2).reshape(SEQ, KVH * HD).astype(jnp.bfloat16))
    return (jnp.stack(outs_all), jnp.stack(gq_all), jnp.stack(gk_all), jnp.stack(gv_all))
```

```python
import math

import jax
import jax.numpy as jnp
from jax import lax
from jax.experimental import pallas as pl
from jax.experimental.pallas import tpu as pltpu
from jax.sharding import PartitionSpec as P

HD = 128
TILE = 128
BT = 8
NB = 16
SL = 8
GROUP = 2
SLOTS = 32
INV_ROOT = 1.0 / math.sqrt(HD)
SCORE_SCALE = INV_ROOT * math.log2(math.e)
FLOOR = -1e30

NT = (((1,), (1,)), ((), ()))


def dot(a, b):
    return jnp.dot(a, b, preferred_element_type=jnp.float32)


def dot_nt(a, b):
    return lax.dot_general(a, b, NT, preferred_element_type=jnp.float32)


def block_of(order_ref, index):
    return lax.shift_right_logical(order_ref[index * BT], 3)


def invert_blocks(order_ref, where_ref):
    for k in range(NB):
        where_ref[block_of(order_ref, k)] = k


def gather_kernel(order_ref, pieces_ref, out_ref, where_ref):
    invert_blocks(order_ref, where_ref)

    @pl.loop(0, NB)
    def _(k):
        b = block_of(order_ref, k)
        for j in range(3):
            src = jnp.maximum(b - 1 - j, 0) if j < 2 else 0
            out_ref[k, j] = pieces_ref[where_ref[src]]


def sum_kernel(order_ref, parts_ref, out_ref, where_ref):
    invert_blocks(order_ref, where_ref)

    @pl.loop(0, NB)
    def _(k):
        b = block_of(order_ref, k)
        near = parts_ref[where_ref[jnp.minimum(b + 1, NB - 1)], 0].astype(jnp.float32)
        far = parts_ref[where_ref[jnp.minimum(b + 2, NB - 1)], 1].astype(jnp.float32)
        total = jnp.where(b + 1 < NB, near, 0.0) + jnp.where(b + 2 < NB, far, 0.0)
        out_ref[k] = total.astype(jnp.bfloat16)

    first = where_ref[0]
    total = parts_ref[where_ref[1], 0].astype(jnp.float32)
    total = total + parts_ref[where_ref[2], 1].astype(jnp.float32)
    for b in range(3, NB):
        total = total + parts_ref[where_ref[b], 2].astype(jnp.float32)
    out_ref[first] = total.astype(jnp.bfloat16)


def attend_kernel(
    order_ref, mask_ref, rows_ref, far_ref, out_ref, dfar_ref,
    k_s, v_s, kt_s, vt_s, s_buf, dk_s, dv_s, dq_s, mask_s, list_s, count_s, sem,
):
    b = block_of(order_ref, lax.axis_index("blk"))
    copy = pltpu.make_async_copy(mask_ref.at[pl.ds(pl.multiple_of(b * BT, BT), BT)], mask_s, sem)
    copy.start()
    dk_s[...] = jnp.zeros_like(dk_s)
    dv_s[...] = jnp.zeros_like(dv_s)

    @pl.loop(0, BT)
    def _(t):
        key = rows_ref[t, :, 512:640]
        value = rows_ref[t, :, 640:768]
        k_s[t] = key
        v_s[t] = value
        kt_s[t] = key.T
        vt_s[t] = value.T

    @pl.loop(0, SLOTS - BT)
    def _(c):
        key = jnp.concatenate([far_ref[0, s, c] for s in range(SL)], axis=0)
        value = jnp.concatenate([far_ref[1, s, c] for s in range(SL)], axis=0)
        k_s[BT + c] = key
        v_s[BT + c] = value
        kt_s[BT + c] = key.T
        vt_s[BT + c] = value.T

    copy.wait()

    @pl.loop(0, BT)
    def _(r):
        count = jnp.int32(0)
        for c in range(SLOTS):
            j, t = divmod(c, BT)
            if j == 0:
                live = (mask_s[r, b * BT + t] == 1) & (t < r)
            elif j < 3:
                live = (mask_s[r, jnp.maximum(b - j, 0) * BT + t] == 1) & (b >= j)
            else:
                live = (mask_s[r, t] == 1) & (b >= 3)
            list_s[r, count] = c
            count = count + live.astype(jnp.int32)
        count_s[r] = count

    q_pos = lax.broadcasted_iota(jnp.int32, (TILE, 2 * TILE), 1) % TILE
    k_pos = lax.broadcasted_iota(jnp.int32, (TILE, 2 * TILE), 0)
    causal = k_pos <= q_pos

    def fold(x, op):
        return op(x.reshape(-1, 8, 2 * TILE), axis=0)

    @pl.loop(0, BT)
    def _(r):
        def stacked(lo):
            return jnp.concatenate(
                [rows_ref[r, :, lo : lo + HD], rows_ref[r, :, lo + HD : lo + 2 * HD]], axis=0
            )

        query = stacked(0)
        upstream = stacked(256)
        others = count_s[r]
        extra = lax.rem(others, GROUP)
        group_count = lax.div(others, GROUP)

        first_tiles = [r] + [
            jnp.where(u < extra, list_s[r, jnp.minimum(u, SLOTS - 1)], r) for u in range(GROUP - 1)
        ]

        def tiles_of(g):
            return [list_s[r, extra + g * GROUP + u] for u in range(GROUP)]

        def joined(ref, tiles, axis):
            return jnp.concatenate([ref[t] for t in tiles], axis=axis)

        scores = dot_nt(joined(k_s, first_tiles, 0), query) * SCORE_SCALE
        seen = jnp.concatenate(
            [causal] + [jnp.broadcast_to(u < extra, causal.shape) for u in range(GROUP - 1)], axis=0
        )
        scores = jnp.where(seen, scores, FLOOR)
        s_buf[0] = scores

        def score_group(g, top):
            scores = dot_nt(joined(k_s, tiles_of(g), 0), query) * SCORE_SCALE
            s_buf[g + 1] = scores
            return jnp.maximum(top, fold(scores, jnp.max))

        top = lax.fori_loop(0, group_count, score_group, fold(scores, jnp.max))
        top = jnp.max(top, axis=0, keepdims=True)

        def weigh(slot, tiles, carry):
            total, acc = carry
            weights = jnp.exp2(s_buf[slot] - top)
            s_buf[slot] = weights
            acc = acc + dot(joined(vt_s, tiles, 1), weights.astype(jnp.bfloat16))
            return total + fold(weights, jnp.sum), acc

        carry = (jnp.zeros((8, 2 * TILE), jnp.float32), jnp.zeros((HD, 2 * TILE), jnp.float32))
        carry = weigh(0, first_tiles, carry)
        total, acc = lax.fori_loop(0, group_count, lambda g, c: weigh(g + 1, tiles_of(g), c), carry)
        inverse = 1.0 / jnp.sum(total, axis=0, keepdims=True)
        attended_t = (acc * inverse).astype(jnp.bfloat16).astype(jnp.float32)
        up32 = upstream.astype(jnp.float32)
        upstream_t = jnp.concatenate([up32[:TILE].T, up32[TILE:].T], axis=1)
        delta = jnp.sum(attended_t * upstream_t, axis=0, keepdims=True)
        out_ref[r, :, 0:HD] = attended_t[:, :TILE].T.astype(jnp.bfloat16)
        out_ref[r, :, HD : 2 * HD] = attended_t[:, TILE:].T.astype(jnp.bfloat16)

        def gradients(slot, tiles, dq):
            probs = s_buf[slot] * inverse
            grad_probs = dot_nt(joined(v_s, tiles, 0), upstream)
            grad_scores = (probs * (grad_probs - delta)).astype(jnp.bfloat16)
            grad_value = dot(probs.astype(jnp.bfloat16), upstream)
            grad_key = dot(grad_scores, query)
            for u, t in enumerate(tiles):
                dv_s[t] += grad_value[u * TILE : (u + 1) * TILE]
                dk_s[t] += grad_key[u * TILE : (u + 1) * TILE]
            return dq + dot(joined(kt_s, tiles, 1), grad_scores)

        dq = gradients(0, first_tiles, jnp.zeros((HD, 2 * TILE), jnp.float32))
        dq = lax.fori_loop(0, group_count, lambda g, c: gradients(g + 1, tiles_of(g), c), dq)
        dq = dq * INV_ROOT
        out_ref[r, :, 256 : 256 + HD] = dq[:, :TILE].T.astype(jnp.bfloat16)
        out_ref[r, :, 256 + HD : 512] = dq[:, TILE:].T.astype(jnp.bfloat16)

    @pl.loop(0, BT)
    def _(t):
        out_ref[t, :, 512:640] = (dk_s[t] * INV_ROOT).astype(jnp.bfloat16)
        out_ref[t, :, 640:768] = dv_s[t].astype(jnp.bfloat16)

    @pl.loop(0, SLOTS - BT)
    def _(c):
        grad_key = (dk_s[BT + c] * INV_ROOT).astype(jnp.bfloat16)
        grad_value = dv_s[BT + c].astype(jnp.bfloat16)
        for s in range(SL):
            dfar_ref[0, s, c] = grad_key[s * 16 : (s + 1) * 16]
            dfar_ref[1, s, c] = grad_value[s * 16 : (s + 1) * 16]


VMEM = pl.BlockSpec(memory_space=pltpu.VMEM)
SMEM = pl.BlockSpec(memory_space=pltpu.SMEM)
ANY = pl.BlockSpec(memory_space=pl.ANY)


def attend(order, mask, rows, far):
    bf16, f32 = jnp.bfloat16, jnp.float32
    tiles = (SLOTS, TILE, HD)
    return pl.pallas_call(
        attend_kernel,
        out_shape=(
            jax.ShapeDtypeStruct((BT, TILE, 768), bf16),
            jax.ShapeDtypeStruct((2, SL, 24, 16, HD), bf16),
        ),
        in_specs=[SMEM, ANY, VMEM, VMEM],
        out_specs=(VMEM, VMEM),
        scratch_shapes=[
            pltpu.VMEM(tiles, bf16),
            pltpu.VMEM(tiles, bf16),
            pltpu.VMEM(tiles, bf16),
            pltpu.VMEM(tiles, bf16),
            pltpu.VMEM((SLOTS // GROUP + 1, GROUP * TILE, 2 * TILE), f32),
            pltpu.VMEM(tiles, f32),
            pltpu.VMEM(tiles, f32),
            pltpu.VMEM((HD, 2 * TILE), f32),
            pltpu.SMEM((BT, 128), jnp.int32),
            pltpu.SMEM((BT, SLOTS + 1), jnp.int32),
            pltpu.SMEM((BT,), jnp.int32),
            pltpu.SemaphoreType.DMA,
        ],
        compiler_params=pltpu.CompilerParams(vmem_limit_bytes=40 * 1024 * 1024),
        cost_estimate=pl.CostEstimate(flops=20_000_000_000, bytes_accessed=6_000_000, transcendentals=0),
    )(order, mask, rows, far)


def routed(kernel, order, array, out_shape):
    return pl.pallas_call(
        kernel,
        out_shape=jax.ShapeDtypeStruct(out_shape, jnp.bfloat16),
        in_specs=[SMEM, VMEM],
        out_specs=VMEM,
        scratch_shapes=[pltpu.SMEM((NB,), jnp.int32)],
        compiler_params=pltpu.CompilerParams(vmem_limit_bytes=16 * 1024 * 1024),
    )(order, array)


def swap(array, axis):
    return lax.all_to_all(array, axis, split_axis=0, concat_axis=0, tiled=True)


def on_device(queries, keys, values, upstream, tile_mask, tile_order):
    order = tile_order[0]
    mask = tile_mask[0]
    by_head = jnp.concatenate(
        [
            queries.reshape(TILE, 8, 256),
            upstream.reshape(TILE, 8, 256),
            jnp.repeat(keys.reshape(TILE, 4, HD), 2, axis=1),
            jnp.repeat(values.reshape(TILE, 4, HD), 2, axis=1),
        ],
        axis=2,
    ).transpose(1, 0, 2)
    rows = swap(by_head, "head")
    pair = rows[:, :, 512:].reshape(BT, SL, 16, 2, HD).transpose(3, 1, 0, 2, 4)
    pieces = swap(pair.reshape(NB, BT, 16, HD), "blk")
    chosen = routed(gather_kernel, order, pieces, (NB, 3, BT, 16, HD))
    far = swap(chosen, "blk").reshape(2, SL, 24, 16, HD)
    out, dfar = attend(order, mask, rows, far)
    parts = swap(dfar.reshape(NB, 3, BT, 16, HD), "blk")
    summed = routed(sum_kernel, order, parts, (NB, BT, 16, HD))
    home = swap(summed, "blk").reshape(2, SL, BT, 16, HD)
    home = home.transpose(2, 1, 3, 0, 4).reshape(BT, TILE, 256)
    pair_out = (out[:, :, 512:].astype(jnp.float32) + home.astype(jnp.float32)).astype(jnp.bfloat16)
    back = swap(jnp.concatenate([out[:, :, :512], pair_out], axis=2), "head")
    attended = back[:, :, :256].transpose(1, 0, 2).reshape(1, TILE, 2048)
    grad_queries = back[:, :, 256:512].transpose(1, 0, 2).reshape(1, TILE, 2048)
    grads = back[:, :, 512:].astype(jnp.float32).reshape(4, 2, TILE, 2, HD).sum(axis=1)
    grads = grads.astype(jnp.bfloat16).transpose(2, 1, 0, 3).reshape(2, 1, TILE, 512)
    return (attended, grad_queries, grads[0], grads[1])


def solution(mesh):
    split = P(None, ("blk", "head"), None)
    return jax.shard_map(
        on_device,
        mesh=mesh,
        in_specs=(split, split, split, split, P(), P()),
        out_specs=(split, split, split, split),
        check_vma=False,
    )
```

```python
import math

import jax
import jax.numpy as jnp
from jax import lax
from jax.experimental import pallas as pl
from jax.experimental.pallas import tpu as pltpu
from jax.sharding import PartitionSpec as P

HD = 128
TILE = 128
WIDE = 256
BT = 8
NB = 16
FAR = 24
WORK = 8
REST = 4
INV_ROOT = 1.0 / math.sqrt(HD)
SCORE_SCALE = INV_ROOT * math.log2(math.e)
FLOOR = -1e30

OWN_COUNT, FAR_COUNT, OWN_LIST, FAR_LIST, PLAN = 0, 1, 8, 16, 64

NT = (((1,), (1,)), ((), ()))


def dot(a, b):
    return jnp.dot(a, b, preferred_element_type=jnp.float32)


def dot_nt(a, b):
    return lax.dot_general(a, b, NT, preferred_element_type=jnp.float32)


def block_of(order_ref, index):
    return lax.shift_right_logical(order_ref[index * BT], 3)


def invert_blocks(order_ref, where_ref):
    for k in range(NB):
        where_ref[block_of(order_ref, k)] = k


def pack_kernel(q_ref, d_ref, k_ref, v_ref, out_ref):
    for u in range(2):
        cols = slice(u * WIDE, (u + 1) * WIDE)
        out_ref[u, :, 0:256] = q_ref[:, cols]
        out_ref[u, :, 256:512] = d_ref[:, cols]
        out_ref[u, :, 512:640] = k_ref[...]
        out_ref[u, :, 640:768] = v_ref[...]


def unpack_kernel(back_ref, o_ref, dq_ref, dk_ref, dv_ref):
    for u in range(2):
        cols = slice(u * WIDE, (u + 1) * WIDE)
        o_ref[:, cols] = back_ref[u, :, 0:256]
        dq_ref[:, cols] = back_ref[u, :, 256:512]

    def both(lo):
        a = back_ref[0, :, lo : lo + HD].astype(jnp.float32)
        return (a + back_ref[1, :, lo : lo + HD].astype(jnp.float32)).astype(jnp.bfloat16)

    dk_ref[...] = both(512)
    dv_ref[...] = both(640)


def add_kernel(pair_ref, home_ref, out_ref):
    for part in range(2):
        cols = slice(part * HD, (part + 1) * HD)
        own = pair_ref[:, :, cols].astype(jnp.float32)
        out_ref[:, :, cols] = (own + home_ref[part].astype(jnp.float32)).astype(jnp.bfloat16)


def gather_kernel(order_ref, pieces_ref, out_ref, where_ref):
    invert_blocks(order_ref, where_ref)

    @pl.loop(0, NB)
    def _(k):
        b = block_of(order_ref, k)
        for j in range(3):
            src = jnp.maximum(b - 1 - j, 0) if j < 2 else 0
            out_ref[k, j] = pieces_ref[where_ref[src]]


def sum_kernel(order_ref, parts_ref, out_ref, where_ref):
    invert_blocks(order_ref, where_ref)

    @pl.loop(0, NB)
    def _(k):
        b = block_of(order_ref, k)
        near = parts_ref[where_ref[jnp.minimum(b + 1, NB - 1)], 0].astype(jnp.float32)
        far = parts_ref[where_ref[jnp.minimum(b + 2, NB - 1)], 1].astype(jnp.float32)
        total = jnp.where(b + 1 < NB, near, 0.0) + jnp.where(b + 2 < NB, far, 0.0)
        out_ref[k] = total.astype(jnp.bfloat16)

    total = parts_ref[where_ref[1], 0].astype(jnp.float32)
    total = total + parts_ref[where_ref[2], 1].astype(jnp.float32)
    for b in range(3, NB):
        total = total + parts_ref[where_ref[b], 2].astype(jnp.float32)
    out_ref[where_ref[0]] = total.astype(jnp.bfloat16)


def fold(x, op):
    return op(x.reshape(-1, 8, WIDE), axis=0)


def spread(x):
    return jnp.broadcast_to(x, (8, WIDE))


def joined(refs, axis):
    return jnp.concatenate(refs, axis=axis)


def stacked(rows_ref, r, lo):
    return joined([rows_ref[r, :, lo : lo + HD], rows_ref[r, :, lo + HD : lo + 2 * HD]], 0)


def own_seen(count):
    k_pos = lax.broadcasted_iota(jnp.int32, (BT * TILE, WIDE), 0)
    q_pos = lax.broadcasted_iota(jnp.int32, (BT * TILE, WIDE), 1) % TILE
    limit = jnp.where(k_pos < TILE, q_pos + 1, (count + 1) * TILE)
    return k_pos < limit


def own_tiles(plan_ref, r):
    count = plan_ref[r, OWN_COUNT]
    rest = [jnp.where(u < count, plan_ref[r, OWN_LIST + u], r) for u in range(BT - 1)]
    return count, [r] + rest


def near_kernel(order_ref, mask_ref, rows_ref, plan_ref, top_ref, total_ref, acc_ref, upt_ref, vt_s, mask_s, sem):
    b = block_of(order_ref, lax.axis_index("blk"))
    copy = pltpu.make_async_copy(mask_ref.at[pl.ds(pl.multiple_of(b * BT, BT), BT)], mask_s, sem)
    copy.start()

    @pl.loop(0, BT)
    def _(t):
        vt_s[t] = rows_ref[t, :, 640:768].T

    copy.wait()

    @pl.loop(0, BT)
    def _(r):
        own = jnp.int32(0)
        for t in range(BT - 1):
            plan_ref[r, OWN_LIST + own] = t
            own = own + ((mask_s[r, b * BT + t] == 1) & (t < r)).astype(jnp.int32)
        plan_ref[r, OWN_COUNT] = own
        far = jnp.int32(0)
        for t in range(BT):
            for j in range(3):
                column = jnp.maximum(b - 1 - j, 0) * BT + t if j < 2 else t
                plan_ref[r, FAR_LIST + far] = t * 3 + j
                far = far + ((mask_s[r, column] == 1) & (b > j)).astype(jnp.int32)
        plan_ref[r, FAR_COUNT] = far

    @pl.loop(0, BT)
    def _(r):
        query = stacked(rows_ref, r, 0)
        count, tiles = own_tiles(plan_ref, r)
        scores = dot_nt(joined([rows_ref[t, :, 512:640] for t in tiles], 0), query) * SCORE_SCALE
        scores = jnp.where(own_seen(count), scores, FLOOR)
        top = jnp.max(fold(scores, jnp.max), axis=0, keepdims=True)
        weights = jnp.exp2(scores - top)
        top_ref[r] = spread(top)
        total_ref[r] = fold(weights, jnp.sum)
        acc_ref[r] = dot(joined([vt_s[t] for t in tiles], 1), weights.astype(jnp.bfloat16))
        upt_ref[r] = joined([rows_ref[r, :, 256:384].T, rows_ref[r, :, 384:512].T], 1)


def far_steps(plan_ref, r, step):
    count = plan_ref[r, FAR_COUNT]
    whole = lax.shift_right_logical(count, 3)
    rest = count & (WORK - 1)

    @pl.loop(0, whole)
    def _(g):
        step(g * WORK, [plan_ref[r, FAR_LIST + g * WORK + u] for u in range(WORK)], None)

    def partly(width):
        base = whole * WORK
        tiles = [
            jnp.where(u < rest, plan_ref[r, FAR_LIST + jnp.minimum(base + u, FAR - 1)], 0)
            for u in range(width)
        ]
        step(base, tiles, rest)

    @pl.when(rest > REST)
    def _():
        partly(WORK)

    @pl.when((rest > 0) & (rest <= REST))
    def _():
        partly(REST)


def only(scores, live):
    if live is None:
        return scores
    row = lax.broadcasted_iota(jnp.int32, scores.shape, 0)
    return jnp.where(row < live * TILE, scores, FLOOR)


def far_kernel(
    plan_ref, rows_ref, far_ref, top_ref, total_ref, acc_ref, upt_ref,
    dfar_ref, ot_ref, lse_ref, delta_ref,
    vt_s, s_buf, dk_s, dv_s, top_s, total_s, acc_s,
):
    dk_s[...] = jnp.zeros_like(dk_s)
    dv_s[...] = jnp.zeros_like(dv_s)

    @pl.loop(0, FAR, unroll=4)
    def _(c):
        vt_s[c] = far_ref[1, c].T

    @pl.loop(0, BT)
    def _(r):
        query = stacked(rows_ref, r, 0)
        upstream = stacked(rows_ref, r, 256)
        top_s[...] = top_ref[r]

        def score(slot, tiles, live):
            width = len(tiles)
            scores = dot_nt(joined([far_ref[0, t] for t in tiles], 0), query) * SCORE_SCALE
            scores = only(scores, live)
            s_buf[pl.ds(slot, width)] = scores.reshape(width, TILE, WIDE)
            top_s[...] = jnp.maximum(top_s[...], fold(scores, jnp.max))

        far_steps(plan_ref, r, score)
        near_top = top_ref[r][:1]
        top = jnp.max(top_s[...], axis=0, keepdims=True)
        shrink = jnp.exp2(near_top - top)
        total_s[...] = total_ref[r] * shrink
        acc_s[...] = acc_ref[r] * shrink

        def weigh(slot, tiles, live):
            width = len(tiles)
            weights = jnp.exp2(s_buf[pl.ds(slot, width)].reshape(width * TILE, WIDE) - top)
            s_buf[pl.ds(slot, width)] = weights.reshape(width, TILE, WIDE)
            total_s[...] += fold(weights, jnp.sum)
            acc_s[...] += dot(joined([vt_s[t] for t in tiles], 1), weights.astype(jnp.bfloat16))

        far_steps(plan_ref, r, weigh)
        total = jnp.sum(total_s[...], axis=0, keepdims=True)
        inverse = 1.0 / total
        attended = (acc_s[...] * inverse).astype(jnp.bfloat16)
        ot_ref[r] = attended
        delta = attended.astype(jnp.float32) * upt_ref[r].astype(jnp.float32)
        delta = jnp.sum(fold(delta, jnp.sum), axis=0, keepdims=True)
        lse_ref[r] = spread(top + jnp.log2(total))
        delta_ref[r] = spread(delta)

        def gradients(slot, tiles, live):
            width = len(tiles)
            probs = s_buf[pl.ds(slot, width)].reshape(width * TILE, WIDE) * inverse
            grad_probs = dot_nt(joined([far_ref[1, t] for t in tiles], 0), upstream)
            grad_scores = (probs * (grad_probs - delta)).astype(jnp.bfloat16)
            grad_value = dot(probs.astype(jnp.bfloat16), upstream)
            grad_key = dot(grad_scores, query)
            for u, t in enumerate(tiles):
                dv_s[t] += grad_value[u * TILE : (u + 1) * TILE]
                dk_s[t] += grad_key[u * TILE : (u + 1) * TILE]

        far_steps(plan_ref, r, gradients)

    dfar_ref[0] = (dk_s[...] * INV_ROOT).astype(jnp.bfloat16)
    dfar_ref[1] = dv_s[...].astype(jnp.bfloat16)


def rest_kernel(
    plan_ref, rows_ref, far_ref, ot_ref, lse_ref, delta_ref, out_ref,
    kt_s, fkt_s, dk_s, dv_s, dq_s,
):
    dk_s[...] = jnp.zeros_like(dk_s)
    dv_s[...] = jnp.zeros_like(dv_s)

    @pl.loop(0, BT)
    def _(t):
        kt_s[t] = rows_ref[t, :, 512:640].T

    @pl.loop(0, FAR, unroll=4)
    def _(c):
        fkt_s[c] = far_ref[0, c].T

    @pl.loop(0, BT)
    def _(r):
        query = stacked(rows_ref, r, 0)
        upstream = stacked(rows_ref, r, 256)
        lse = lse_ref[r][:1]
        delta = delta_ref[r][:1]
        attended = ot_ref[r].astype(jnp.float32)
        out_ref[r, :, 0:HD] = attended[:, :TILE].T.astype(jnp.bfloat16)
        out_ref[r, :, HD : 2 * HD] = attended[:, TILE:].T.astype(jnp.bfloat16)

        def common(scores, value):
            probs = jnp.exp2(scores - lse)
            grad_probs = dot_nt(value, upstream)
            return probs, (probs * (grad_probs - delta)).astype(jnp.bfloat16)

        count, tiles = own_tiles(plan_ref, r)
        scores = dot_nt(joined([rows_ref[t, :, 512:640] for t in tiles], 0), query) * SCORE_SCALE
        scores = jnp.where(own_seen(count), scores, FLOOR)
        probs, grad_scores = common(scores, joined([rows_ref[t, :, 640:768] for t in tiles], 0))
        grad_value = dot(probs.astype(jnp.bfloat16), upstream)
        grad_key = dot(grad_scores, query)
        for u, t in enumerate(tiles):
            dv_s[t] += grad_value[u * TILE : (u + 1) * TILE]
            dk_s[t] += grad_key[u * TILE : (u + 1) * TILE]
        dq_s[...] = dot(joined([kt_s[t] for t in tiles], 1), grad_scores)

        def queries(slot, tiles, live):
            scores = dot_nt(joined([far_ref[0, t] for t in tiles], 0), query) * SCORE_SCALE
            _, grad_scores = common(only(scores, live), joined([far_ref[1, t] for t in tiles], 0))
            dq_s[...] += dot(joined([fkt_s[t] for t in tiles], 1), grad_scores)

        far_steps(plan_ref, r, queries)
        dq = dq_s[...] * INV_ROOT
        out_ref[r, :, 256 : 256 + HD] = dq[:, :TILE].T.astype(jnp.bfloat16)
        out_ref[r, :, 256 + HD : 512] = dq[:, TILE:].T.astype(jnp.bfloat16)

    @pl.loop(0, BT)
    def _(t):
        out_ref[t, :, 512:640] = (dk_s[t] * INV_ROOT).astype(jnp.bfloat16)
        out_ref[t, :, 640:768] = dv_s[t].astype(jnp.bfloat16)


VMEM = pl.BlockSpec(memory_space=pltpu.VMEM)
SMEM = pl.BlockSpec(memory_space=pltpu.SMEM)
ANY = pl.BlockSpec(memory_space=pl.ANY)
BF16, F32 = jnp.bfloat16, jnp.float32


def shape(dims, dtype):
    return jax.ShapeDtypeStruct(dims, dtype)


def limit(mib):
    return pltpu.CompilerParams(vmem_limit_bytes=mib * 1024 * 1024)


def cost(us):
    return pl.CostEstimate(flops=us * 1_000_000_000, bytes_accessed=us * 100_000, transcendentals=0)


def pack(queries, upstream, keys, values):
    wide = pl.BlockSpec((TILE, 512), lambda g: (0, g))
    slim = pl.BlockSpec((TILE, HD), lambda g: (0, g))
    return pl.pallas_call(
        pack_kernel,
        grid=(4,),
        out_shape=shape((8, TILE, 768), BF16),
        in_specs=[wide, wide, slim, slim],
        out_specs=pl.BlockSpec((2, TILE, 768), lambda g: (g, 0, 0)),
    )(queries, upstream, keys, values)


def unpack(back):
    wide = pl.BlockSpec((TILE, 512), lambda g: (0, g))
    slim = pl.BlockSpec((TILE, HD), lambda g: (0, g))
    return pl.pallas_call(
        unpack_kernel,
        grid=(4,),
        out_shape=(shape((TILE, 2048), BF16),) * 2 + (shape((TILE, 512), BF16),) * 2,
        in_specs=[pl.BlockSpec((2, TILE, 768), lambda g: (g, 0, 0))],
        out_specs=(wide, wide, slim, slim),
    )(back)


def add_home(out, home):
    pair = pl.BlockSpec((BT, TILE, 256), lambda g: (0, 0, 2))
    return pl.pallas_call(
        add_kernel,
        grid=(1,),
        out_shape=shape((BT, TILE, 768), BF16),
        in_specs=[pair, pl.BlockSpec((2, BT, TILE, HD), lambda g: (0, 0, 0, 0))],
        out_specs=pair,
        input_output_aliases={0: 0},
    )(out, home)


def near(order, mask, rows):
    return pl.pallas_call(
        near_kernel,
        out_shape=(
            shape((BT, PLAN), jnp.int32),
            shape((BT, 8, WIDE), F32),
            shape((BT, 8, WIDE), F32),
            shape((BT, HD, WIDE), F32),
            shape((BT, HD, WIDE), BF16),
        ),
        in_specs=[SMEM, ANY, VMEM],
        out_specs=(SMEM, VMEM, VMEM, VMEM, VMEM),
        scratch_shapes=[
            pltpu.VMEM((BT, HD, TILE), BF16),
            pltpu.SMEM((BT, 128), jnp.int32),
            pltpu.SemaphoreType.DMA,
        ],
        compiler_params=limit(32),
        cost_estimate=cost(12),
    )(order, mask, rows)


def far_part(plan, rows, far, top, total, acc, upt):
    return pl.pallas_call(
        far_kernel,
        out_shape=(
            shape((2, FAR, TILE, HD), BF16),
            shape((BT, HD, WIDE), BF16),
            shape((BT, 8, WIDE), F32),
            shape((BT, 8, WIDE), F32),
        ),
        in_specs=[SMEM] + [VMEM] * 6,
        out_specs=(VMEM,) * 4,
        scratch_shapes=[
            pltpu.VMEM((FAR, HD, TILE), BF16),
            pltpu.VMEM((FAR, TILE, WIDE), F32),
            pltpu.VMEM((FAR, TILE, HD), F32),
            pltpu.VMEM((FAR, TILE, HD), F32),
            pltpu.VMEM((8, WIDE), F32),
            pltpu.VMEM((8, WIDE), F32),
            pltpu.VMEM((HD, WIDE), F32),
        ],
        compiler_params=limit(40),
        cost_estimate=cost(25),
    )(plan, rows, far, top, total, acc, upt)


def rest_part(plan, rows, far, ot, lse, delta):
    return pl.pallas_call(
        rest_kernel,
        out_shape=shape((BT, TILE, 768), BF16),
        in_specs=[SMEM] + [VMEM] * 5,
        out_specs=VMEM,
        scratch_shapes=[
            pltpu.VMEM((BT, HD, TILE), BF16),
            pltpu.VMEM((FAR, HD, TILE), BF16),
            pltpu.VMEM((BT, TILE, HD), F32),
            pltpu.VMEM((BT, TILE, HD), F32),
            pltpu.VMEM((HD, WIDE), F32),
        ],
        compiler_params=limit(40),
        cost_estimate=cost(25),
    )(plan, rows, far, ot, lse, delta)


def routed(kernel, order, array, out_shape):
    return pl.pallas_call(
        kernel,
        out_shape=shape(out_shape, BF16),
        in_specs=[SMEM, VMEM],
        out_specs=VMEM,
        scratch_shapes=[pltpu.SMEM((NB,), jnp.int32)],
        compiler_params=limit(16),
    )(order, array)


def swap(array, axis):
    return lax.all_to_all(array, axis, split_axis=0, concat_axis=0, tiled=True)


def on_device(queries, keys, values, upstream, tile_mask, tile_order):
    order = tile_order[0]
    rows = swap(pack(queries[0], upstream[0], keys[0], values[0]), "head")
    pair = rows[:, :, 512:].reshape(BT, TILE, 2, HD).transpose(2, 0, 1, 3)
    pieces = swap(pair.reshape(NB, TILE, HD), "blk")
    chosen = routed(gather_kernel, order, pieces, (NB, 3, TILE, HD))
    far = swap(chosen, "blk").reshape(2, FAR, TILE, HD)
    plan, top, total, acc, upt = near(order, tile_mask[0], rows)
    dfar, ot, lse, delta = far_part(plan, rows, far, top, total, acc, upt)
    parts = swap(dfar.reshape(NB, 3, TILE, HD), "blk")
    out = rest_part(plan, rows, far, ot, lse, delta)
    parts, out = lax.optimization_barrier((parts, out))
    summed = routed(sum_kernel, order, parts, (NB, TILE, HD))
    home = swap(summed, "blk").reshape(2, BT, TILE, HD)
    back = swap(add_home(out, home), "head")
    return tuple(array[None] for array in unpack(back))


def solution(mesh):
    split = P(None, ("blk", "head"), None)
    return jax.shard_map(
        on_device,
        mesh=mesh,
        in_specs=(split, split, split, split, P(), P()),
        out_specs=(split, split, split, split),
        check_vma=False,
    )
```

```python
import functools
import math

import jax
import jax.numpy as jnp
from jax import lax
from jax.experimental import pallas as pl
from jax.experimental.pallas import tpu as pltpu
from jax.sharding import PartitionSpec as P

HD = 128
TILE = 128
WIDE = 256
BT = 8
NB = 16
FAR = 24
HALF = 64
EARLY = 4
WORK = 8
REST = 4
STEP = 4
INV_ROOT = 1.0 / math.sqrt(HD)
SCORE_SCALE = INV_ROOT * math.log2(math.e)
FLOOR = -1e30

OWN_COUNT, FAR_COUNT, OWN_LIST, FAR_LIST, PLAN = 0, 1, 8, 16, 64

NT = (((1,), (1,)), ((), ()))


def dot(a, b):
    return jnp.dot(a, b, preferred_element_type=jnp.float32)


def dot_nt(a, b):
    return lax.dot_general(a, b, NT, preferred_element_type=jnp.float32)


def block_of(order_ref, index):
    return lax.shift_right_logical(order_ref[index * BT], 3)


def invert_blocks(order_ref, where_ref):
    for k in range(NB):
        where_ref[block_of(order_ref, k)] = k


def core():
    return lax.axis_index("blk") & 1


def served_block():
    return (lax.axis_index("blk") & ~1) + lax.shift_right_logical(lax.axis_index("head"), 2)


def pair_columns(group, which):
    return pl.ds(pl.multiple_of((2 * group + which) * WIDE, WIDE), WIDE)


def pack_kernel(*refs):
    sources, (keep_ref, send_ref), landed, sems = refs[:4], refs[4:6], refs[6:10], refs[10]
    copies = [
        pltpu.make_async_copy(source, target, sems.at[n])
        for n, (source, target) in enumerate(zip(sources, landed))
    ]
    for copy in copies:
        copy.start()
    for copy in copies:
        copy.wait()
    q_ref, d_ref, k_ref, v_ref = landed
    me = core()
    for g in range(4):
        for ref, which in ((keep_ref, me), (send_ref, 1 - me)):
            ref[g, :, 0:256] = q_ref[:, pair_columns(g, which)]
            ref[g, :, 256:512] = d_ref[:, pair_columns(g, which)]
        key = k_ref[:, g * HD : (g + 1) * HD]
        value = v_ref[:, g * HD : (g + 1) * HD]
        keep_ref[g, :, 512:640] = jnp.where(me == 0, key, value)
        send_ref[g, :, 512:640] = jnp.where(me == 0, value, key)


def merge_kernel(keep_ref, came_ref, out_ref):
    me = core()
    for g in range(4):
        out_ref[me * 4 + g] = keep_ref[g]
        out_ref[(1 - me) * 4 + g] = came_ref[g]


def pick_kernel(back_ref, send_ref):
    for g in range(4):
        send_ref[g] = back_ref[(1 - core()) * 4 + g]


def unpack_kernel(back_ref, came_ref, o_ref, dq_ref, dk_ref, dv_ref):
    me = core()
    for g in range(4):
        mine = back_ref[me * 4 + g]
        for piece, which in ((mine, me), (came_ref[g], 1 - me)):
            o_ref[:, pair_columns(g, which)] = piece[:, 0:256]
            dq_ref[:, pair_columns(g, which)] = piece[:, 256:512]
        a, b = mine[:, 512:640], came_ref[g, :, 512:640]
        dk_ref[:, g * HD : (g + 1) * HD] = jnp.where(me == 0, a, b)
        dv_ref[:, g * HD : (g + 1) * HD] = jnp.where(me == 0, b, a)


def pair_sum_kernel(keep_ref, came_ref, out_ref):
    total = keep_ref[...].astype(jnp.float32) + came_ref[...].astype(jnp.float32)
    out_ref[...] = total.astype(jnp.bfloat16)


def add_kernel(rows_ref, late_ref, keep_ref, came_ref, home_ref, out_ref):
    out_ref[EARLY:, :, 256:512] = late_ref[...]
    total = keep_ref[...] + came_ref[...].astype(jnp.float32) + home_ref[...].astype(jnp.float32)
    out_ref[:, :, 512:640] = total.astype(jnp.bfloat16)


def gather_kernel(order_ref, pieces_ref, out_ref, where_ref):
    invert_blocks(order_ref, where_ref)

    @pl.loop(0, NB)
    def _(k):
        b = block_of(order_ref, k)
        for j in range(3):
            src = jnp.maximum(b - 1 - j, 0) if j < 2 else 0
            out_ref[k, j] = pieces_ref[where_ref[src]]


def sum_kernel(order_ref, parts_ref, out_ref, where_ref):
    invert_blocks(order_ref, where_ref)

    @pl.loop(0, NB)
    def _(k):
        b = block_of(order_ref, k)
        near = parts_ref[where_ref[jnp.minimum(b + 1, NB - 1)], 0].astype(jnp.float32)
        far = parts_ref[where_ref[jnp.minimum(b + 2, NB - 1)], 1].astype(jnp.float32)
        total = jnp.where(b + 1 < NB, near, 0.0) + jnp.where(b + 2 < NB, far, 0.0)
        out_ref[k] = total.astype(jnp.bfloat16)

    total = parts_ref[where_ref[1], 0].astype(jnp.float32)
    total = total + parts_ref[where_ref[2], 1].astype(jnp.float32)
    for b in range(3, NB):
        total = total + parts_ref[where_ref[b], 2].astype(jnp.float32)
    out_ref[where_ref[0]] = total.astype(jnp.bfloat16)


def fold(x, op):
    return op(x.reshape(-1, 8, WIDE), axis=0)


def spread(x):
    return jnp.broadcast_to(x, (8, WIDE))


def joined(refs, axis):
    return jnp.concatenate(refs, axis=axis)


def stacked(rows_ref, r, lo):
    return joined([rows_ref[r, :, lo : lo + HD], rows_ref[r, :, lo + HD : lo + 2 * HD]], 0)


def own_seen(count):
    k_pos = lax.broadcasted_iota(jnp.int32, (BT * TILE, WIDE), 0)
    q_pos = lax.broadcasted_iota(jnp.int32, (BT * TILE, WIDE), 1) % TILE
    limit = jnp.where(k_pos < TILE, q_pos + 1, (count + 1) * TILE)
    return k_pos < limit


def own_tiles(plan_ref, r):
    count = plan_ref[r, OWN_COUNT]
    rest = [jnp.where(u < count, plan_ref[r, OWN_LIST + u], r) for u in range(BT - 1)]
    return count, [r] + rest


def near_kernel(
    order_ref, mask_ref, rows_ref, came_ref, plan_ref, top_ref, total_ref, acc_ref, upt_ref,
    own_s, vt_s, mask_s, sem,
):
    b = block_of(order_ref, served_block())
    copy = pltpu.make_async_copy(mask_ref.at[pl.ds(pl.multiple_of(b * BT, BT), BT)], mask_s, sem)
    copy.start()

    @pl.loop(0, BT)
    def _(t):
        own_s[core(), t] = rows_ref[t, :, 512:640]
        own_s[1 - core(), t] = came_ref[t]
        vt_s[t] = own_s[1, t].T

    copy.wait()

    @pl.loop(0, BT)
    def _(r):
        own = jnp.int32(0)
        for t in range(BT - 1):
            plan_ref[r, OWN_LIST + own] = t
            own = own + ((mask_s[r, b * BT + t] == 1) & (t < r)).astype(jnp.int32)
        plan_ref[r, OWN_COUNT] = own
        far = jnp.int32(0)
        for t in range(BT):
            for j in range(3):
                column = jnp.maximum(b - 1 - j, 0) * BT + t if j < 2 else t
                plan_ref[r, FAR_LIST + far] = t * 6 + j
                far = far + ((mask_s[r, column] == 1) & (b > j)).astype(jnp.int32)
        plan_ref[r, FAR_COUNT] = far

    @pl.loop(0, BT)
    def _(r):
        query = stacked(rows_ref, r, 0)
        count, tiles = own_tiles(plan_ref, r)
        scores = dot_nt(joined([own_s[0, t] for t in tiles], 0), query) * SCORE_SCALE
        scores = jnp.where(own_seen(count), scores, FLOOR)
        top = jnp.max(fold(scores, jnp.max), axis=0, keepdims=True)
        weights = jnp.exp2(scores - top)
        top_ref[r] = spread(top)
        total_ref[r] = fold(weights, jnp.sum)
        acc_ref[r] = dot(joined([vt_s[t] for t in tiles], 1), weights.astype(jnp.bfloat16))
        upt_ref[r] = joined([rows_ref[r, :, 256:384].T, rows_ref[r, :, 384:512].T], 1)


def far_steps(plan_ref, r, step):
    count = plan_ref[r, FAR_COUNT]
    whole = lax.shift_right_logical(count, 3)
    rest = count & (WORK - 1)

    @pl.loop(0, whole)
    def _(g):
        step(g * WORK, [plan_ref[r, FAR_LIST + g * WORK + u] for u in range(WORK)], None)

    def partly(width):
        base = whole * WORK
        tiles = [
            jnp.where(u < rest, plan_ref[r, FAR_LIST + jnp.minimum(base + u, FAR - 1)], 0)
            for u in range(width)
        ]
        step(base, tiles, rest)

    @pl.when(rest > REST)
    def _():
        partly(WORK)

    @pl.when((rest > 0) & (rest <= REST))
    def _():
        partly(REST)


def halves(ref, part, tiles):
    return [ref[part, t + 3 * half] for t in tiles for half in range(2)]


def only(scores, live):
    if live is None:
        return scores
    row = lax.broadcasted_iota(jnp.int32, scores.shape, 0)
    return jnp.where(row < live * TILE, scores, FLOOR)


def far_kernel(
    plan_ref, rows_ref, far_ref, came_ref, top_ref, total_ref, acc_ref, upt_ref,
    keep_ref, send_ref, ot_ref, lse_ref, delta_ref,
    kv_s, vt_s, s_buf, dk_s, dv_s,
):
    dk_s[...] = jnp.zeros_like(dk_s)
    dv_s[...] = jnp.zeros_like(dv_s)
    kv_s[core()] = far_ref[...]
    kv_s[1 - core()] = came_ref[...]

    @pl.loop(0, BT)
    def _(t):
        for j in range(3):
            vt_s[t * 6 + j] = joined(halves(kv_s, 1, [t * 6 + j]), 0).T

    def work(r, width):
        count = plan_ref[r, FAR_COUNT]
        listed = [plan_ref[r, FAR_LIST + u] for u in range(width)]
        sure = width - STEP
        tiles = [t if u <= sure else jnp.where(u < count, t, 0) for u, t in enumerate(listed)]
        query = stacked(rows_ref, r, 0)
        upstream_t = upt_ref[r].astype(jnp.float32)
        near_top = top_ref[r][:1]
        top = near_top
        if width:
            scores = dot_nt(joined(halves(kv_s, 0, tiles), 0), query) * SCORE_SCALE
            row = lax.broadcasted_iota(jnp.int32, (STEP * TILE, WIDE), 0)
            last = jnp.where(row < (count - sure) * TILE, scores[sure * TILE :], FLOOR)
            scores = joined([scores[: sure * TILE], last], 0) if sure else last
            s_buf[: width * TILE] = scores
            top = jnp.maximum(top, jnp.max(fold(scores, jnp.max), axis=0, keepdims=True))
        shrink = jnp.exp2(near_top - top)
        total = total_ref[r] * shrink
        acc = acc_ref[r] * shrink
        if width:
            weights = jnp.exp2(s_buf[: width * TILE] - top)
            s_buf[: width * TILE] = weights
            total = total + fold(weights, jnp.sum)
            acc = acc + dot(joined([vt_s[t] for t in tiles], 1), weights.astype(jnp.bfloat16))
        total = jnp.sum(total, axis=0, keepdims=True)
        inverse = 1.0 / total
        attended = (acc * inverse).astype(jnp.bfloat16)
        ot_ref[r] = attended
        delta = attended.astype(jnp.float32) * upstream_t
        delta = jnp.sum(fold(delta, jnp.sum), axis=0, keepdims=True)
        lse_ref[r] = spread(top + jnp.log2(total))
        delta_ref[r] = spread(delta)
        if width:
            probs = s_buf[: width * TILE] * inverse
            grad_probs = dot(joined(halves(kv_s, 1, tiles), 0), upt_ref[r])
            grad_scores = (probs * (grad_probs - delta)).astype(jnp.bfloat16)
            grad_value = dot_nt(probs.astype(jnp.bfloat16), upt_ref[r])
            grad_key = dot(grad_scores, query)
            for u, t in enumerate(tiles):
                for half in range(2):
                    part = slice(u * TILE + half * HALF, u * TILE + (half + 1) * HALF)
                    dv_s[t + 3 * half] += grad_value[part]
                    dk_s[t + 3 * half] += grad_key[part]

    dk_s[...] = jnp.zeros_like(dk_s)
    dv_s[...] = jnp.zeros_like(dv_s)

    @pl.loop(0, BT)
    def _(r):
        steps = lax.shift_right_logical(plan_ref[r, FAR_COUNT] + STEP - 1, 2)
        for width in range(0, FAR + 1, STEP):
            pl.when(steps == width // STEP)(functools.partial(work, r, width))

    grad_key = (dk_s[...] * INV_ROOT).astype(jnp.bfloat16)
    grad_value = dv_s[...].astype(jnp.bfloat16)
    keep_ref[...] = jnp.where(core() == 0, grad_key, grad_value)
    send_ref[...] = jnp.where(core() == 0, grad_value, grad_key)


def score_gradients(scores, value, upstream, lse, delta):
    probs = jnp.exp2(scores - lse)
    grad_probs = dot_nt(value, upstream)
    return probs, (probs * (grad_probs - delta)).astype(jnp.bfloat16)


def far_queries(plan_ref, kv_s, fkt_s, dq_s, r, query, upstream, lse, delta):
    def step(slot, tiles, live):
        scores = only(dot_nt(joined(halves(kv_s, 0, tiles), 0), query) * SCORE_SCALE, live)
        value = joined(halves(kv_s, 1, tiles), 0)
        _, grad_scores = score_gradients(scores, value, upstream, lse, delta)
        dq_s[...] += dot(joined([fkt_s[t] for t in tiles], 1), grad_scores)

    far_steps(plan_ref, r, step)


def turned(dq_s):
    dq = dq_s[...] * INV_ROOT
    return joined([dq[:, :TILE].T, dq[:, TILE:].T], 1).astype(jnp.bfloat16)


def rest_kernel(
    plan_ref, rows_ref, other_ref, far_ref, came_ref, ot_ref, lse_ref, delta_ref,
    out_ref, keep_ref, send_ref, part_ref,
    own_s, kv_s, kt_s, fkt_s, dk_s, dv_s, dq_s,
):
    dk_s[...] = jnp.zeros_like(dk_s)
    dv_s[...] = jnp.zeros_like(dv_s)
    kv_s[core()] = far_ref[...]
    kv_s[1 - core()] = came_ref[...]

    @pl.loop(0, BT)
    def _(t):
        own_s[core(), t] = rows_ref[t, :, 512:640]
        own_s[1 - core(), t] = other_ref[t]
        kt_s[t] = own_s[0, t].T
        for j in range(3):
            fkt_s[t * 6 + j] = joined(halves(kv_s, 0, [t * 6 + j]), 0).T

    @pl.loop(0, BT)
    def _(r):
        query = stacked(rows_ref, r, 0)
        upstream = stacked(rows_ref, r, 256)
        lse = lse_ref[r][:1]
        delta = delta_ref[r][:1]
        attended = ot_ref[r].astype(jnp.float32)
        out_ref[r, :, 0:HD] = attended[:, :TILE].T.astype(jnp.bfloat16)
        out_ref[r, :, HD : 2 * HD] = attended[:, TILE:].T.astype(jnp.bfloat16)

        count, tiles = own_tiles(plan_ref, r)
        scores = dot_nt(joined([own_s[0, t] for t in tiles], 0), query) * SCORE_SCALE
        scores = jnp.where(own_seen(count), scores, FLOOR)
        probs, grad_scores = score_gradients(
            scores, joined([own_s[1, t] for t in tiles], 0), upstream, lse, delta
        )
        grad_value = dot(probs.astype(jnp.bfloat16), upstream)
        grad_key = dot(grad_scores, query)
        for u, t in enumerate(tiles):
            dv_s[t] += grad_value[u * TILE : (u + 1) * TILE]
            dk_s[t] += grad_key[u * TILE : (u + 1) * TILE]
        dq_s[...] = dot(joined([kt_s[t] for t in tiles], 1), grad_scores)

        @pl.when(r < EARLY)
        def _():
            far_queries(plan_ref, kv_s, fkt_s, dq_s, r, query, upstream, lse, delta)
            out_ref[r, :, 256:512] = turned(dq_s)

        @pl.when(r >= EARLY)
        def _():
            part_ref[r - EARLY] = dq_s[...]

    grad_key = dk_s[...] * INV_ROOT
    grad_value = dv_s[...]
    keep_ref[...] = jnp.where(core() == 0, grad_key, grad_value)
    send_ref[...] = jnp.where(core() == 0, grad_value, grad_key).astype(jnp.bfloat16)


def late_kernel(
    plan_ref, rows_ref, far_ref, came_ref, lse_ref, delta_ref, part_ref, late_ref, kv_s, fkt_s, dq_s
):
    kv_s[core()] = far_ref[...]
    kv_s[1 - core()] = came_ref[...]

    @pl.loop(0, BT)
    def _(t):
        for j in range(3):
            fkt_s[t * 6 + j] = joined(halves(kv_s, 0, [t * 6 + j]), 0).T

    @pl.loop(EARLY, BT)
    def _(r):
        query = stacked(rows_ref, r, 0)
        upstream = stacked(rows_ref, r, 256)
        dq_s[...] = part_ref[r - EARLY]
        far_queries(
            plan_ref, kv_s, fkt_s, dq_s, r, query, upstream, lse_ref[r][:1], delta_ref[r][:1]
        )
        late_ref[r - EARLY] = turned(dq_s)


VMEM = pl.BlockSpec(memory_space=pltpu.VMEM)
SMEM = pl.BlockSpec(memory_space=pltpu.SMEM)
ANY = pl.BlockSpec(memory_space=pl.ANY)
HBM = pl.BlockSpec(memory_space=pltpu.HBM)
BF16, F32 = jnp.bfloat16, jnp.float32


def shape(dims, dtype):
    return jax.ShapeDtypeStruct(dims, dtype)


def limit(mib):
    return pltpu.CompilerParams(vmem_limit_bytes=mib * 1024 * 1024)


def cost(us):
    return pl.CostEstimate(flops=us * 1_000_000_000, bytes_accessed=us * 100_000, transcendentals=0)


def pack(queries, upstream, keys, values):
    return pl.pallas_call(
        pack_kernel,
        out_shape=(shape((4, TILE, 640), BF16),) * 2,
        in_specs=[ANY] * 4,
        out_specs=(VMEM, VMEM),
        scratch_shapes=[
            pltpu.VMEM((TILE, 2048), BF16),
            pltpu.VMEM((TILE, 2048), BF16),
            pltpu.VMEM((TILE, 512), BF16),
            pltpu.VMEM((TILE, 512), BF16),
            pltpu.SemaphoreType.DMA((4,)),
        ],
        compiler_params=limit(60),
    )(queries, upstream, keys, values)


def simple(kernel, out_shape, *arrays):
    return pl.pallas_call(
        kernel,
        out_shape=out_shape,
        in_specs=[VMEM] * len(arrays),
        out_specs=jax.tree.map(lambda _: VMEM, out_shape),
        compiler_params=limit(16),
    )(*arrays)


def add_home(out, late, keep, came, home):
    return pl.pallas_call(
        add_kernel,
        out_shape=shape((BT, TILE, 640), BF16),
        in_specs=[VMEM] * 5,
        out_specs=VMEM,
        input_output_aliases={0: 0},
        compiler_params=limit(16),
    )(out, late, keep, came, home)


def near(order, mask, rows, other):
    return pl.pallas_call(
        near_kernel,
        out_shape=(
            shape((BT, PLAN), jnp.int32),
            shape((BT, 8, WIDE), F32),
            shape((BT, 8, WIDE), F32),
            shape((BT, HD, WIDE), F32),
            shape((BT, HD, WIDE), BF16),
        ),
        in_specs=[SMEM, ANY, VMEM, VMEM],
        out_specs=(SMEM, VMEM, VMEM, VMEM, VMEM),
        scratch_shapes=[
            pltpu.VMEM((2, BT, TILE, HD), BF16),
            pltpu.VMEM((BT, HD, TILE), BF16),
            pltpu.SMEM((BT, 128), jnp.int32),
            pltpu.SemaphoreType.DMA,
        ],
        compiler_params=limit(60),
        cost_estimate=cost(12),
    )(order, mask, rows, other)


def far_part(plan, rows, far, came, top, total, acc, upt):
    return pl.pallas_call(
        far_kernel,
        out_shape=(
            shape((2 * FAR, HALF, HD), BF16),
            shape((2 * FAR, HALF, HD), BF16),
            shape((BT, HD, WIDE), BF16),
            shape((BT, 8, WIDE), F32),
            shape((BT, 8, WIDE), F32),
        ),
        in_specs=[SMEM] + [VMEM] * 7,
        out_specs=(VMEM,) * 5,
        scratch_shapes=[
            pltpu.VMEM((2, 2 * FAR, HALF, HD), BF16),
            pltpu.VMEM((2 * FAR, HD, TILE), BF16),
            pltpu.VMEM((FAR * TILE, WIDE), F32),
            pltpu.VMEM((2 * FAR, HALF, HD), F32),
            pltpu.VMEM((2 * FAR, HALF, HD), F32),
        ],
        compiler_params=limit(60),
        cost_estimate=cost(25),
    )(plan, rows, far, came, top, total, acc, upt)


def rest_part(plan, rows, other, far, came, ot, lse, delta):
    return pl.pallas_call(
        rest_kernel,
        out_shape=(
            shape((BT, TILE, 640), BF16),
            shape((BT, TILE, HD), F32),
            shape((BT, TILE, HD), BF16),
            shape((BT - EARLY, HD, WIDE), F32),
        ),
        in_specs=[SMEM] + [VMEM] * 7,
        out_specs=(VMEM,) * 4,
        scratch_shapes=[
            pltpu.VMEM((2, BT, TILE, HD), BF16),
            pltpu.VMEM((2, 2 * FAR, HALF, HD), BF16),
            pltpu.VMEM((BT, HD, TILE), BF16),
            pltpu.VMEM((2 * FAR, HD, TILE), BF16),
            pltpu.VMEM((BT, TILE, HD), F32),
            pltpu.VMEM((BT, TILE, HD), F32),
            pltpu.VMEM((HD, WIDE), F32),
        ],
        compiler_params=limit(60),
        cost_estimate=cost(18),
    )(plan, rows, other, far, came, ot, lse, delta)


def late_part(plan, rows, far, came, lse, delta, part):
    return pl.pallas_call(
        late_kernel,
        out_shape=shape((BT - EARLY, TILE, WIDE), BF16),
        in_specs=[SMEM] + [VMEM] * 6,
        out_specs=VMEM,
        scratch_shapes=[
            pltpu.VMEM((2, 2 * FAR, HALF, HD), BF16),
            pltpu.VMEM((2 * FAR, HD, TILE), BF16),
            pltpu.VMEM((HD, WIDE), F32),
        ],
        compiler_params=limit(60),
        cost_estimate=cost(10),
    )(plan, rows, far, came, lse, delta, part)


def routed(kernel, order, array, out_shape):
    return pl.pallas_call(
        kernel,
        out_shape=shape(out_shape, BF16),
        in_specs=[SMEM, VMEM],
        out_specs=VMEM,
        scratch_shapes=[pltpu.SMEM((NB,), jnp.int32)],
        compiler_params=limit(16),
    )(order, array)


def over_heads(array):
    return lax.all_to_all(array, "head", split_axis=0, concat_axis=0, tiled=True)


SERVING = [
    [(2 * chip + u) * 8 + beta * 4 + g for chip in range(8) for beta in range(2)]
    for u in range(2)
    for g in range(4)
]


def over_blocks(array):
    return lax.all_to_all(
        array, ("blk", "head"), split_axis=0, concat_axis=0, axis_index_groups=SERVING, tiled=True
    )


def to_other_core(array):
    return lax.ppermute(array, "blk", [(i, i ^ 1) for i in range(16)])


def on_device(queries, keys, values, upstream, tile_mask, tile_order):
    order = tile_order[0]
    keep, send = pack(queries[0], upstream[0], keys[0], values[0])
    both = simple(merge_kernel, shape((8, TILE, 640), BF16), keep, to_other_core(send))
    rows = over_heads(both)
    own = rows[:, :, 512:]
    other = to_other_core(own)
    pieces = over_blocks(own.reshape(NB, HALF, HD))
    chosen = routed(gather_kernel, order, pieces, (NB, 3, HALF, HD))
    far = over_blocks(chosen).reshape(2 * FAR, HALF, HD)
    begun = near(order, tile_mask[0], rows, other)
    far, *begun = lax.optimization_barrier((far, *begun))
    plan = begun[0]
    came = to_other_core(far)
    keep, send, ot, lse, delta = far_part(plan, rows, far, came, *begun[1:])
    dfar = simple(pair_sum_kernel, shape((2 * FAR, HALF, HD), BF16), keep, to_other_core(send))
    parts = over_blocks(dfar.reshape(NB, 3, HALF, HD))
    out, keep, send, part = rest_part(plan, rows, other, far, came, ot, lse, delta)
    parts, out, keep, send, part = lax.optimization_barrier((parts, out, keep, send, part))
    summed = routed(sum_kernel, order, parts, (NB, HALF, HD))
    summed, part = lax.optimization_barrier((summed, part))
    home = over_blocks(summed).reshape(BT, TILE, HD)
    late = late_part(plan, rows, far, came, lse, delta, part)
    back = over_heads(add_home(out, late, keep, to_other_core(send), home))
    came = to_other_core(simple(pick_kernel, shape((4, TILE, 640), BF16), back))
    wide, slim = shape((TILE, 2048), BF16), shape((TILE, 512), BF16)
    outs = simple(unpack_kernel, (wide, wide, slim, slim), back, came)
    return tuple(array[None] for array in outs)


def solution(mesh):
    split = P(None, ("blk", "head"), None)
    return jax.shard_map(
        on_device,
        mesh=mesh,
        in_specs=(split, split, split, split, P(), P()),
        out_specs=(split, split, split, split),
        check_vma=False,
    )
```

```python
import functools
import math

import jax
import jax.numpy as jnp
from jax import lax
from jax.experimental import pallas as pl
from jax.experimental.pallas import tpu as pltpu
from jax.sharding import PartitionSpec as P

HD = 128
TILE = 128
WIDE = 256
BT = 8
NB = 16
FAR = 24
HALF = 64
EARLY = 5
WORK = 8
REST = 4
SUB = 4
STEP = 4
INV_ROOT = 1.0 / math.sqrt(HD)
SCORE_SCALE = INV_ROOT * math.log2(math.e)
FLOOR = -1e30

OWN_COUNT, FAR_COUNT, OWN_LIST, FAR_LIST, PLAN = 0, 1, 8, 16, 64

NT = (((1,), (1,)), ((), ()))


def dot(a, b):
    return jnp.dot(a, b, preferred_element_type=jnp.float32)


def dot_nt(a, b):
    return lax.dot_general(a, b, NT, preferred_element_type=jnp.float32)


def block_of(order_ref, index):
    return lax.shift_right_logical(order_ref[index * BT], 3)


def invert_blocks(order_ref, where_ref):
    for k in range(NB):
        where_ref[block_of(order_ref, k)] = k


def core():
    return lax.axis_index("blk") & 1


def served_block():
    return (lax.axis_index("blk") & ~1) + lax.shift_right_logical(lax.axis_index("head"), 2)


def pair_columns(group, which):
    return pl.ds(pl.multiple_of((2 * group + which) * WIDE, WIDE), WIDE)


def pack_kernel(*refs):
    sources, (keep_ref, send_ref), landed, sems = refs[:4], refs[4:6], refs[6:10], refs[10]
    copies = [
        pltpu.make_async_copy(source, target, sems.at[n])
        for n, (source, target) in enumerate(zip(sources, landed))
    ]
    for copy in copies:
        copy.start()
    for copy in copies:
        copy.wait()
    q_ref, d_ref, k_ref, v_ref = landed
    me = core()
    for g in range(4):
        for ref, which in ((keep_ref, me), (send_ref, 1 - me)):
            ref[g, :, 0:256] = q_ref[:, pair_columns(g, which)]
            ref[g, :, 256:512] = d_ref[:, pair_columns(g, which)]
        key = k_ref[:, g * HD : (g + 1) * HD]
        value = v_ref[:, g * HD : (g + 1) * HD]
        keep_ref[g, :, 512:640] = jnp.where(me == 0, key, value)
        send_ref[g, :, 512:640] = jnp.where(me == 0, value, key)


def merge_kernel(keep_ref, came_ref, out_ref):
    me = core()
    for g in range(4):
        out_ref[me * 4 + g] = keep_ref[g]
        out_ref[(1 - me) * 4 + g] = came_ref[g]


def pick_kernel(back_ref, send_ref):
    for g in range(4):
        send_ref[g] = back_ref[(1 - core()) * 4 + g]


def unpack_kernel(back_ref, came_ref, o_ref, dq_ref, dk_ref, dv_ref):
    me = core()
    for g in range(4):
        mine = back_ref[me * 4 + g]
        for piece, which in ((mine, me), (came_ref[g], 1 - me)):
            o_ref[:, pair_columns(g, which)] = piece[:, 0:256]
            dq_ref[:, pair_columns(g, which)] = piece[:, 256:512]
        a, b = mine[:, 512:640], came_ref[g, :, 512:640]
        dk_ref[:, g * HD : (g + 1) * HD] = jnp.where(me == 0, a, b)
        dv_ref[:, g * HD : (g + 1) * HD] = jnp.where(me == 0, b, a)


def pair_sum_kernel(keep_ref, came_ref, out_ref):
    total = keep_ref[...].astype(jnp.float32) + came_ref[...].astype(jnp.float32)
    out_ref[...] = total.astype(jnp.bfloat16)


def add_kernel(rows_ref, late_ref, keep_ref, came_ref, home_ref, out_ref):
    out_ref[EARLY:, :, 256:512] = late_ref[...]
    total = keep_ref[...] + came_ref[...].astype(jnp.float32) + home_ref[...].astype(jnp.float32)
    out_ref[:, :, 512:640] = total.astype(jnp.bfloat16)


def gather_kernel(order_ref, pieces_ref, out_ref, where_ref):
    invert_blocks(order_ref, where_ref)

    @pl.loop(0, NB)
    def _(k):
        b = block_of(order_ref, k)
        for j in range(3):
            src = jnp.maximum(b - 1 - j, 0) if j < 2 else 0
            out_ref[k, j] = pieces_ref[where_ref[src]]


def sum_kernel(order_ref, parts_ref, out_ref, where_ref):
    invert_blocks(order_ref, where_ref)

    @pl.loop(0, NB)
    def _(k):
        b = block_of(order_ref, k)
        near = parts_ref[where_ref[jnp.minimum(b + 1, NB - 1)], 0].astype(jnp.float32)
        far = parts_ref[where_ref[jnp.minimum(b + 2, NB - 1)], 1].astype(jnp.float32)
        total = jnp.where(b + 1 < NB, near, 0.0) + jnp.where(b + 2 < NB, far, 0.0)
        out_ref[k] = total.astype(jnp.bfloat16)

    total = parts_ref[where_ref[1], 0].astype(jnp.float32)
    total = total + parts_ref[where_ref[2], 1].astype(jnp.float32)
    for b in range(3, NB):
        total = total + parts_ref[where_ref[b], 2].astype(jnp.float32)
    out_ref[where_ref[0]] = total.astype(jnp.bfloat16)


def fold(x, op):
    return op(x.reshape(-1, 8, WIDE), axis=0)


def spread(x):
    return jnp.broadcast_to(x, (8, WIDE))


def joined(refs, axis):
    return jnp.concatenate(refs, axis=axis)


def stacked(rows_ref, r, lo):
    return joined([rows_ref[r, :, lo : lo + HD], rows_ref[r, :, lo + HD : lo + 2 * HD]], 0)


def own_seen(count, width):
    k_pos = lax.broadcasted_iota(jnp.int32, (width * TILE, WIDE), 0)
    q_pos = lax.broadcasted_iota(jnp.int32, (width * TILE, WIDE), 1) % TILE
    limit = jnp.where(k_pos < TILE, q_pos + 1, (count + 1) * TILE)
    return k_pos < limit


def own_tiles(plan_ref, r, width):
    count = plan_ref[r, OWN_COUNT]
    rest = [jnp.where(u < count, plan_ref[r, OWN_LIST + u], r) for u in range(width - 1)]
    return count, [r] + rest


def near_kernel(
    order_ref, mask_ref, rows_ref, came_ref, plan_ref, top_ref, total_ref, acc_ref, upt_ref, qs_ref,
    own_s, vt_s, mask_s, sem,
):
    b = block_of(order_ref, served_block())
    copy = pltpu.make_async_copy(mask_ref.at[pl.ds(pl.multiple_of(b * BT, BT), BT)], mask_s, sem)
    copy.start()

    @pl.loop(0, BT)
    def _(t):
        own_s[core(), t] = rows_ref[t, :, 512:640]
        own_s[1 - core(), t] = came_ref[t]
        vt_s[t] = own_s[1, t].T

    copy.wait()

    @pl.loop(0, BT)
    def _(r):
        own = jnp.int32(0)
        for t in range(BT - 1):
            plan_ref[r, OWN_LIST + own] = t
            own = own + ((mask_s[r, b * BT + t] == 1) & (t < r)).astype(jnp.int32)
        plan_ref[r, OWN_COUNT] = own
        far = jnp.int32(0)
        for t in range(BT):
            for j in range(3):
                column = jnp.maximum(b - 1 - j, 0) * BT + t if j < 2 else t
                plan_ref[r, FAR_LIST + far] = t * 6 + j
                far = far + ((mask_s[r, column] == 1) & (b > j)).astype(jnp.int32)
        plan_ref[r, FAR_COUNT] = far

    @pl.loop(0, BT)
    def _(r):
        query = stacked(rows_ref, r, 0)
        qs_ref[r] = query
        count, tiles = own_tiles(plan_ref, r, BT)
        scores = dot_nt(joined([own_s[0, t] for t in tiles], 0), query) * SCORE_SCALE
        scores = jnp.where(own_seen(count, BT), scores, FLOOR)
        top = jnp.max(fold(scores, jnp.max), axis=0, keepdims=True)
        weights = jnp.exp2(scores - top)
        top_ref[r] = spread(top)
        total_ref[r] = fold(weights, jnp.sum)
        acc_ref[r] = dot(joined([vt_s[t] for t in tiles], 1), weights.astype(jnp.bfloat16))
        upt_ref[r] = joined([rows_ref[r, :, 256:384].T, rows_ref[r, :, 384:512].T], 1)


def far_steps(plan_ref, r, step):
    count = plan_ref[r, FAR_COUNT]
    whole = lax.shift_right_logical(count, 3)
    rest = count & (WORK - 1)

    @pl.loop(0, whole)
    def _(g):
        step(g * WORK, [plan_ref[r, FAR_LIST + g * WORK + u] for u in range(WORK)], None)

    def partly(width):
        base = whole * WORK
        tiles = [
            jnp.where(u < rest, plan_ref[r, FAR_LIST + jnp.minimum(base + u, FAR - 1)], 0)
            for u in range(width)
        ]
        step(base, tiles, rest)

    @pl.when(rest > REST)
    def _():
        partly(WORK)

    @pl.when((rest > 0) & (rest <= REST))
    def _():
        partly(REST)


def halves(ref, part, tiles):
    return [ref[part, t + 3 * half] for t in tiles for half in range(2)]


def only(scores, live):
    if live is None:
        return scores
    row = lax.broadcasted_iota(jnp.int32, scores.shape, 0)
    return jnp.where(row < live * TILE, scores, FLOOR)


def far_kernel(
    plan_ref, far_ref, came_ref, top_ref, total_ref, acc_ref, upt_ref, qs_ref,
    keep_ref, send_ref, ot_ref, lse_ref, delta_ref,
    kv_s, vt_s, s_buf, w_buf, dk_s, dv_s,
):
    dk_s[...] = jnp.zeros_like(dk_s)
    dv_s[...] = jnp.zeros_like(dv_s)
    kv_s[core()] = far_ref[...]
    kv_s[1 - core()] = came_ref[...]

    @pl.loop(0, BT)
    def _(t):
        for j in range(3):
            vt_s[t * 6 + j] = joined(halves(kv_s, 1, [t * 6 + j]), 0).T

    def work(r, width):
        count = plan_ref[r, FAR_COUNT]
        listed = [plan_ref[r, FAR_LIST + u] for u in range(width)]
        sure = width - STEP
        tiles = [t if u <= sure else jnp.where(u < count, t, 0) for u, t in enumerate(listed)]
        parts = [(lo, min(lo + SUB, width)) for lo in range(0, width, SUB)]
        query = qs_ref[r]
        upstream = upt_ref[r]
        near_top = top_ref[r][:1]
        tops = top_ref[r]
        for lo, hi in parts:
            scores = dot_nt(joined(halves(kv_s, 0, tiles[lo:hi]), 0), query) * SCORE_SCALE
            if hi > sure + 1:
                scores = only(scores, count - lo)
            s_buf[lo * TILE : hi * TILE] = scores
            tops = jnp.maximum(tops, fold(scores, jnp.max))
        top = jnp.max(tops, axis=0, keepdims=True)
        shrink = jnp.exp2(near_top - top)
        total = total_ref[r] * shrink
        acc = acc_ref[r] * shrink
        for lo, hi in parts:
            weights = jnp.exp2(s_buf[lo * TILE : hi * TILE] - top)
            total = total + fold(weights, jnp.sum)
            w_buf[lo * TILE : hi * TILE] = weights.astype(jnp.bfloat16)
        if width:
            acc = acc + dot(joined([vt_s[t] for t in tiles], 1), w_buf[: width * TILE])
        total = jnp.sum(total, axis=0, keepdims=True)
        attended = (acc * (1.0 / total)).astype(jnp.bfloat16)
        ot_ref[r] = attended
        delta = attended.astype(jnp.float32) * upstream.astype(jnp.float32)
        delta = jnp.sum(fold(delta, jnp.sum), axis=0, keepdims=True)
        lse = top + jnp.log2(total)
        lse_ref[r] = spread(lse)
        delta_ref[r] = spread(delta)
        for lo, hi in parts:
            probs = jnp.exp2(s_buf[lo * TILE : hi * TILE] - lse)
            grad_probs = dot(joined(halves(kv_s, 1, tiles[lo:hi]), 0), upstream)
            grad_scores = (probs * (grad_probs - delta)).astype(jnp.bfloat16)
            grad_value = dot_nt(probs.astype(jnp.bfloat16), upstream)
            grad_key = dot(grad_scores, query)
            for u, t in enumerate(tiles[lo:hi]):
                for half in range(2):
                    part = slice(u * TILE + half * HALF, u * TILE + (half + 1) * HALF)
                    dv_s[t + 3 * half] += grad_value[part]
                    dk_s[t + 3 * half] += grad_key[part]

    dk_s[...] = jnp.zeros_like(dk_s)
    dv_s[...] = jnp.zeros_like(dv_s)

    @pl.loop(0, BT)
    def _(r):
        steps = lax.shift_right_logical(plan_ref[r, FAR_COUNT] + STEP - 1, 2)
        for width in range(0, FAR + 1, STEP):
            pl.when(steps == width // STEP)(functools.partial(work, r, width))

    grad_key = (dk_s[...] * INV_ROOT).astype(jnp.bfloat16)
    grad_value = dv_s[...].astype(jnp.bfloat16)
    keep_ref[...] = jnp.where(core() == 0, grad_key, grad_value)
    send_ref[...] = jnp.where(core() == 0, grad_value, grad_key)


def score_gradients(scores, value, upstream, lse, delta):
    probs = jnp.exp2(scores - lse)
    grad_probs = dot_nt(value, upstream)
    return probs, (probs * (grad_probs - delta)).astype(jnp.bfloat16)


def far_queries(plan_ref, kv_s, fkt_s, dq_s, r, query, upstream, lse, delta):
    def step(slot, tiles, live):
        scores = only(dot_nt(joined(halves(kv_s, 0, tiles), 0), query) * SCORE_SCALE, live)
        value = joined(halves(kv_s, 1, tiles), 0)
        _, grad_scores = score_gradients(scores, value, upstream, lse, delta)
        dq_s[...] += dot(joined([fkt_s[t] for t in tiles], 1), grad_scores)

    far_steps(plan_ref, r, step)


def turned(dq_s):
    dq = dq_s[...] * INV_ROOT
    return joined([dq[:, :TILE].T, dq[:, TILE:].T], 1).astype(jnp.bfloat16)


def rest_kernel(
    plan_ref, rows_ref, other_ref, far_ref, came_ref, ot_ref, lse_ref, delta_ref,
    out_ref, keep_ref, send_ref, part_ref,
    own_s, kv_s, kt_s, fkt_s, dk_s, dv_s, dq_s,
):
    dk_s[...] = jnp.zeros_like(dk_s)
    dv_s[...] = jnp.zeros_like(dv_s)
    kv_s[core()] = far_ref[...]
    kv_s[1 - core()] = came_ref[...]

    @pl.loop(0, BT)
    def _(t):
        own_s[core(), t] = rows_ref[t, :, 512:640]
        own_s[1 - core(), t] = other_ref[t]
        kt_s[t] = own_s[0, t].T
        for j in range(3):
            fkt_s[t * 6 + j] = joined(halves(kv_s, 0, [t * 6 + j]), 0).T

    @pl.loop(0, BT)
    def _(r):
        query = stacked(rows_ref, r, 0)
        upstream = stacked(rows_ref, r, 256)
        lse = lse_ref[r][:1]
        delta = delta_ref[r][:1]
        attended = ot_ref[r].astype(jnp.float32)
        out_ref[r, :, 0:HD] = attended[:, :TILE].T.astype(jnp.bfloat16)
        out_ref[r, :, HD : 2 * HD] = attended[:, TILE:].T.astype(jnp.bfloat16)

        def own(width):
            count, tiles = own_tiles(plan_ref, r, width)
            scores = dot_nt(joined([own_s[0, t] for t in tiles], 0), query) * SCORE_SCALE
            scores = jnp.where(own_seen(count, width), scores, FLOOR)
            probs, grad_scores = score_gradients(
                scores, joined([own_s[1, t] for t in tiles], 0), upstream, lse, delta
            )
            grad_value = dot(probs.astype(jnp.bfloat16), upstream)
            grad_key = dot(grad_scores, query)
            for u, t in enumerate(tiles):
                dv_s[t] += grad_value[u * TILE : (u + 1) * TILE]
                dk_s[t] += grad_key[u * TILE : (u + 1) * TILE]
            dq_s[...] = dot(joined([kt_s[t] for t in tiles], 1), grad_scores)

        pairs = lax.shift_right_logical(plan_ref[r, OWN_COUNT] + 2, 1)
        for width in range(2, BT + 1, 2):
            pl.when(pairs == width // 2)(functools.partial(own, width))

        @pl.when(r < EARLY)
        def _():
            far_queries(plan_ref, kv_s, fkt_s, dq_s, r, query, upstream, lse, delta)
            out_ref[r, :, 256:512] = turned(dq_s)

        @pl.when(r >= EARLY)
        def _():
            part_ref[r - EARLY] = dq_s[...]

    grad_key = dk_s[...] * INV_ROOT
    grad_value = dv_s[...]
    keep_ref[...] = jnp.where(core() == 0, grad_key, grad_value)
    send_ref[...] = jnp.where(core() == 0, grad_value, grad_key).astype(jnp.bfloat16)


def late_kernel(
    plan_ref, rows_ref, far_ref, came_ref, lse_ref, delta_ref, part_ref, late_ref, kv_s, fkt_s, dq_s
):
    kv_s[core()] = far_ref[...]
    kv_s[1 - core()] = came_ref[...]

    @pl.loop(0, BT)
    def _(t):
        for j in range(3):
            fkt_s[t * 6 + j] = joined(halves(kv_s, 0, [t * 6 + j]), 0).T

    @pl.loop(EARLY, BT)
    def _(r):
        query = stacked(rows_ref, r, 0)
        upstream = stacked(rows_ref, r, 256)
        dq_s[...] = part_ref[r - EARLY]
        far_queries(
            plan_ref, kv_s, fkt_s, dq_s, r, query, upstream, lse_ref[r][:1], delta_ref[r][:1]
        )
        late_ref[r - EARLY] = turned(dq_s)


VMEM = pl.BlockSpec(memory_space=pltpu.VMEM)
SMEM = pl.BlockSpec(memory_space=pltpu.SMEM)
ANY = pl.BlockSpec(memory_space=pl.ANY)
HBM = pl.BlockSpec(memory_space=pltpu.HBM)
BF16, F32 = jnp.bfloat16, jnp.float32


def shape(dims, dtype):
    return jax.ShapeDtypeStruct(dims, dtype)


def limit(mib):
    return pltpu.CompilerParams(vmem_limit_bytes=mib * 1024 * 1024)


def cost(us):
    return pl.CostEstimate(flops=us * 1_000_000_000, bytes_accessed=us * 100_000, transcendentals=0)


def pack(queries, upstream, keys, values):
    return pl.pallas_call(
        pack_kernel,
        out_shape=(shape((4, TILE, 640), BF16),) * 2,
        in_specs=[ANY] * 4,
        out_specs=(VMEM, VMEM),
        scratch_shapes=[
            pltpu.VMEM((TILE, 2048), BF16),
            pltpu.VMEM((TILE, 2048), BF16),
            pltpu.VMEM((TILE, 512), BF16),
            pltpu.VMEM((TILE, 512), BF16),
            pltpu.SemaphoreType.DMA((4,)),
        ],
        compiler_params=limit(60),
    )(queries, upstream, keys, values)


def simple(kernel, out_shape, *arrays):
    return pl.pallas_call(
        kernel,
        out_shape=out_shape,
        in_specs=[VMEM] * len(arrays),
        out_specs=jax.tree.map(lambda _: VMEM, out_shape),
        compiler_params=limit(16),
    )(*arrays)


def add_home(out, late, keep, came, home):
    return pl.pallas_call(
        add_kernel,
        out_shape=shape((BT, TILE, 640), BF16),
        in_specs=[VMEM] * 5,
        out_specs=VMEM,
        input_output_aliases={0: 0},
        compiler_params=limit(16),
    )(out, late, keep, came, home)


def near(order, mask, rows, other):
    return pl.pallas_call(
        near_kernel,
        out_shape=(
            shape((BT, PLAN), jnp.int32),
            shape((BT, 8, WIDE), F32),
            shape((BT, 8, WIDE), F32),
            shape((BT, HD, WIDE), F32),
            shape((BT, HD, WIDE), BF16),
            shape((BT, WIDE, HD), BF16),
        ),
        in_specs=[SMEM, ANY, VMEM, VMEM],
        out_specs=(SMEM, VMEM, VMEM, VMEM, VMEM, VMEM),
        scratch_shapes=[
            pltpu.VMEM((2, BT, TILE, HD), BF16),
            pltpu.VMEM((BT, HD, TILE), BF16),
            pltpu.SMEM((BT, 128), jnp.int32),
            pltpu.SemaphoreType.DMA,
        ],
        compiler_params=limit(60),
        cost_estimate=cost(12),
    )(order, mask, rows, other)


def far_part(plan, far, came, top, total, acc, upt, qs):
    return pl.pallas_call(
        far_kernel,
        out_shape=(
            shape((2 * FAR, HALF, HD), BF16),
            shape((2 * FAR, HALF, HD), BF16),
            shape((BT, HD, WIDE), BF16),
            shape((BT, 8, WIDE), F32),
            shape((BT, 8, WIDE), F32),
        ),
        in_specs=[SMEM] + [VMEM] * 7,
        out_specs=(VMEM,) * 5,
        scratch_shapes=[
            pltpu.VMEM((2, 2 * FAR, HALF, HD), BF16),
            pltpu.VMEM((2 * FAR, HD, TILE), BF16),
            pltpu.VMEM((FAR * TILE, WIDE), F32),
            pltpu.VMEM((FAR * TILE, WIDE), BF16),
            pltpu.VMEM((2 * FAR, HALF, HD), F32),
            pltpu.VMEM((2 * FAR, HALF, HD), F32),
        ],
        compiler_params=limit(60),
        cost_estimate=cost(25),
    )(plan, far, came, top, total, acc, upt, qs)


def rest_part(plan, rows, other, far, came, ot, lse, delta):
    return pl.pallas_call(
        rest_kernel,
        out_shape=(
            shape((BT, TILE, 640), BF16),
            shape((BT, TILE, HD), F32),
            shape((BT, TILE, HD), BF16),
            shape((BT - EARLY, HD, WIDE), F32),
        ),
        in_specs=[SMEM] + [VMEM] * 7,
        out_specs=(VMEM,) * 4,
        scratch_shapes=[
            pltpu.VMEM((2, BT, TILE, HD), BF16),
            pltpu.VMEM((2, 2 * FAR, HALF, HD), BF16),
            pltpu.VMEM((BT, HD, TILE), BF16),
            pltpu.VMEM((2 * FAR, HD, TILE), BF16),
            pltpu.VMEM((BT, TILE, HD), F32),
            pltpu.VMEM((BT, TILE, HD), F32),
            pltpu.VMEM((HD, WIDE), F32),
        ],
        compiler_params=limit(60),
        cost_estimate=cost(18),
    )(plan, rows, other, far, came, ot, lse, delta)


def late_part(plan, rows, far, came, lse, delta, part):
    return pl.pallas_call(
        late_kernel,
        out_shape=shape((BT - EARLY, TILE, WIDE), BF16),
        in_specs=[SMEM] + [VMEM] * 6,
        out_specs=VMEM,
        scratch_shapes=[
            pltpu.VMEM((2, 2 * FAR, HALF, HD), BF16),
            pltpu.VMEM((2 * FAR, HD, TILE), BF16),
            pltpu.VMEM((HD, WIDE), F32),
        ],
        compiler_params=limit(60),
        cost_estimate=cost(10),
    )(plan, rows, far, came, lse, delta, part)


def routed(kernel, order, array, out_shape):
    return pl.pallas_call(
        kernel,
        out_shape=shape(out_shape, BF16),
        in_specs=[SMEM, VMEM],
        out_specs=VMEM,
        scratch_shapes=[pltpu.SMEM((NB,), jnp.int32)],
        compiler_params=limit(16),
    )(order, array)


def over_heads(array):
    return lax.all_to_all(array, "head", split_axis=0, concat_axis=0, tiled=True)


SERVING = [
    [(2 * chip + u) * 8 + beta * 4 + g for chip in range(8) for beta in range(2)]
    for u in range(2)
    for g in range(4)
]


def over_blocks(array):
    return lax.all_to_all(
        array, ("blk", "head"), split_axis=0, concat_axis=0, axis_index_groups=SERVING, tiled=True
    )


def to_other_core(array):
    return lax.ppermute(array, "blk", [(i, i ^ 1) for i in range(16)])


def on_device(queries, keys, values, upstream, tile_mask, tile_order):
    order = tile_order[0]
    keep, send = pack(queries[0], upstream[0], keys[0], values[0])
    both = simple(merge_kernel, shape((8, TILE, 640), BF16), keep, to_other_core(send))
    rows = over_heads(both)
    own = rows[:, :, 512:]
    other = to_other_core(own)
    pieces = over_blocks(own.reshape(NB, HALF, HD))
    chosen = routed(gather_kernel, order, pieces, (NB, 3, HALF, HD))
    far = over_blocks(chosen).reshape(2 * FAR, HALF, HD)
    begun = near(order, tile_mask[0], rows, other)
    far, *begun = lax.optimization_barrier((far, *begun))
    plan = begun[0]
    came = to_other_core(far)
    keep, send, ot, lse, delta = far_part(plan, far, came, *begun[1:])
    dfar = simple(pair_sum_kernel, shape((2 * FAR, HALF, HD), BF16), keep, to_other_core(send))
    parts = over_blocks(dfar.reshape(NB, 3, HALF, HD))
    out, keep, send, part = rest_part(plan, rows, other, far, came, ot, lse, delta)
    parts, out, keep, send, part = lax.optimization_barrier((parts, out, keep, send, part))
    summed = routed(sum_kernel, order, parts, (NB, HALF, HD))
    summed, part = lax.optimization_barrier((summed, part))
    home = over_blocks(summed).reshape(BT, TILE, HD)
    late = late_part(plan, rows, far, came, lse, delta, part)
    back = over_heads(add_home(out, late, keep, to_other_core(send), home))
    came = to_other_core(simple(pick_kernel, shape((4, TILE, 640), BF16), back))
    wide, slim = shape((TILE, 2048), BF16), shape((TILE, 512), BF16)
    outs = simple(unpack_kernel, (wide, wide, slim, slim), back, came)
    return tuple(array[None] for array in outs)


def solution(mesh):
    split = P(None, ("blk", "head"), None)
    return jax.shard_map(
        on_device,
        mesh=mesh,
        in_specs=(split, split, split, split, P(), P()),
        out_specs=(split, split, split, split),
        check_vma=False,
    )
```

```python
import functools
import math

import jax
import jax.numpy as jnp
from jax import lax
from jax.experimental import pallas as pl
from jax.experimental.pallas import tpu as pltpu
from jax.sharding import PartitionSpec as P

HD = 128
TILE = 128
WIDE = 256
BT = 8
NB = 16
FAR = 24
HALF = 64
EARLY = 5
SUB = 4
STEP = 4
INV_ROOT = 1.0 / math.sqrt(HD)
SCORE_SCALE = INV_ROOT * math.log2(math.e)
FLOOR = -1e30

OWN_COUNT, FAR_COUNT, OWN_LIST, FAR_LIST, PLAN = 0, 1, 8, 16, 64

NT = (((1,), (1,)), ((), ()))


def dot(a, b):
    return jnp.dot(a, b, preferred_element_type=jnp.float32)


def dot_nt(a, b):
    return lax.dot_general(a, b, NT, preferred_element_type=jnp.float32)


def block_of(order_ref, index):
    return lax.shift_right_logical(order_ref[index * BT], 3)


def invert_blocks(order_ref, where_ref):
    for k in range(NB):
        where_ref[block_of(order_ref, k)] = k


def core():
    return lax.axis_index("blk") & 1


def served_block():
    return (lax.axis_index("blk") & ~1) + lax.shift_right_logical(lax.axis_index("head"), 2)


def pair_columns(group, which):
    return pl.ds(pl.multiple_of((2 * group + which) * WIDE, WIDE), WIDE)


def pack_kernel(*refs):
    sources, (keep_ref, send_ref), landed, sems = refs[:4], refs[4:6], refs[6:10], refs[10]
    copies = [
        pltpu.make_async_copy(source, target, sems.at[n])
        for n, (source, target) in enumerate(zip(sources, landed))
    ]
    for copy in copies:
        copy.start()
    for copy in copies:
        copy.wait()
    q_ref, d_ref, k_ref, v_ref = landed
    me = core()
    for g in range(4):
        for ref, which in ((keep_ref, me), (send_ref, 1 - me)):
            ref[g, :, 0:256] = q_ref[:, pair_columns(g, which)]
            ref[g, :, 256:512] = d_ref[:, pair_columns(g, which)]
        key = k_ref[:, g * HD : (g + 1) * HD]
        value = v_ref[:, g * HD : (g + 1) * HD]
        keep_ref[g, :, 512:640] = jnp.where(me == 0, key, value)
        send_ref[g, :, 512:640] = jnp.where(me == 0, value, key)


def merge_kernel(keep_ref, came_ref, out_ref):
    me = core()
    for g in range(4):
        out_ref[me * 4 + g] = keep_ref[g]
        out_ref[(1 - me) * 4 + g] = came_ref[g]


def pick_kernel(back_ref, send_ref):
    for g in range(4):
        send_ref[g] = back_ref[(1 - core()) * 4 + g]


def unpack_kernel(back_ref, came_ref, o_ref, dq_ref, dk_ref, dv_ref):
    me = core()
    for g in range(4):
        mine = back_ref[me * 4 + g]
        for piece, which in ((mine, me), (came_ref[g], 1 - me)):
            o_ref[:, pair_columns(g, which)] = piece[:, 0:256]
            dq_ref[:, pair_columns(g, which)] = piece[:, 256:512]
        a, b = mine[:, 512:640], came_ref[g, :, 512:640]
        dk_ref[:, g * HD : (g + 1) * HD] = jnp.where(me == 0, a, b)
        dv_ref[:, g * HD : (g + 1) * HD] = jnp.where(me == 0, b, a)


def add_kernel(rows_ref, late_ref, keep_ref, came_ref, home_ref, out_ref):
    out_ref[EARLY:, :, 256:512] = late_ref[...]
    total = keep_ref[...] + came_ref[...].astype(jnp.float32) + home_ref[...].astype(jnp.float32)
    out_ref[:, :, 512:640] = total.astype(jnp.bfloat16)


def gather_kernel(order_ref, pieces_ref, out_ref, where_ref):
    invert_blocks(order_ref, where_ref)

    @pl.loop(0, NB)
    def _(k):
        b = block_of(order_ref, k)
        for j in range(3):
            src = jnp.maximum(b - 1 - j, 0) if j < 2 else 0
            out_ref[k, j] = pieces_ref[where_ref[src]]


def sum_kernel(order_ref, parts_ref, out_ref, where_ref):
    invert_blocks(order_ref, where_ref)

    @pl.loop(0, NB)
    def _(k):
        b = block_of(order_ref, k)
        near = parts_ref[where_ref[jnp.minimum(b + 1, NB - 1)], 0].astype(jnp.float32)
        far = parts_ref[where_ref[jnp.minimum(b + 2, NB - 1)], 1].astype(jnp.float32)
        total = jnp.where(b + 1 < NB, near, 0.0) + jnp.where(b + 2 < NB, far, 0.0)
        out_ref[k] = total.astype(jnp.bfloat16)

    total = parts_ref[where_ref[1], 0].astype(jnp.float32)
    total = total + parts_ref[where_ref[2], 1].astype(jnp.float32)
    for b in range(3, NB):
        total = total + parts_ref[where_ref[b], 2].astype(jnp.float32)
    out_ref[where_ref[0]] = total.astype(jnp.bfloat16)


def fold(x, op):
    return op(x.reshape(-1, 8, WIDE), axis=0)


def spread(x):
    return jnp.broadcast_to(x, (8, WIDE))


def joined(refs, axis):
    return jnp.concatenate(refs, axis=axis)


def stacked(rows_ref, r, lo):
    return joined([rows_ref[r, :, lo : lo + HD], rows_ref[r, :, lo + HD : lo + 2 * HD]], 0)


def own_seen(count, lo, hi):
    k_pos = lax.broadcasted_iota(jnp.int32, ((hi - lo) * TILE, WIDE), 0) + lo * TILE
    q_pos = lax.broadcasted_iota(jnp.int32, ((hi - lo) * TILE, WIDE), 1) % TILE
    limit = jnp.where(k_pos < TILE, q_pos + 1, (count + 1) * TILE)
    return k_pos < limit


def own_tiles(plan_ref, r, width):
    count = plan_ref[r, OWN_COUNT]
    rest = [jnp.where(u < count, plan_ref[r, OWN_LIST + u], r) for u in range(width - 1)]
    return count, [r] + rest


def near_kernel(
    order_ref, mask_ref, rows_ref, came_ref, plan_ref, top_ref, total_ref, acc_ref, upt_ref, qs_ref,
    own_s, vt_s, mask_s, sem,
):
    b = block_of(order_ref, served_block())
    copy = pltpu.make_async_copy(mask_ref.at[pl.ds(pl.multiple_of(b * BT, BT), BT)], mask_s, sem)
    copy.start()

    @pl.loop(0, BT)
    def _(t):
        own_s[core(), t] = rows_ref[t, :, 512:640]
        own_s[1 - core(), t] = came_ref[t]
        vt_s[t] = own_s[1, t].T

    copy.wait()

    @pl.loop(0, BT)
    def _(r):
        own = jnp.int32(0)
        for t in range(BT - 1):
            plan_ref[r, OWN_LIST + own] = t
            own = own + ((mask_s[r, b * BT + t] == 1) & (t < r)).astype(jnp.int32)
        plan_ref[r, OWN_COUNT] = own
        far = jnp.int32(0)
        for t in range(BT):
            for j in range(3):
                column = jnp.maximum(b - 1 - j, 0) * BT + t if j < 2 else t
                plan_ref[r, FAR_LIST + far] = t * 6 + j
                far = far + ((mask_s[r, column] == 1) & (b > j)).astype(jnp.int32)
        plan_ref[r, FAR_COUNT] = far

    @pl.loop(0, BT)
    def _(r):
        query = stacked(rows_ref, r, 0)
        qs_ref[r] = query

        def own(width):
            count, tiles = own_tiles(plan_ref, r, width)
            scores = dot_nt(joined([own_s[0, t] for t in tiles], 0), query) * SCORE_SCALE
            scores = jnp.where(own_seen(count, 0, width), scores, FLOOR)
            top = jnp.max(fold(scores, jnp.max), axis=0, keepdims=True)
            weights = jnp.exp2(scores - top)
            top_ref[r] = spread(top)
            total_ref[r] = fold(weights, jnp.sum)
            acc_ref[r] = dot(joined([vt_s[t] for t in tiles], 1), weights.astype(jnp.bfloat16))

        pairs = lax.shift_right_logical(plan_ref[r, OWN_COUNT] + 2, 1)
        for width in range(2, BT + 1, 2):
            pl.when(pairs == width // 2)(functools.partial(own, width))

        upt_ref[r] = joined([rows_ref[r, :, 256:384].T, rows_ref[r, :, 384:512].T], 1)


def halves(ref, part, tiles):
    return [ref[part, t + 3 * half] for t in tiles for half in range(2)]


def only(scores, live):
    row = lax.broadcasted_iota(jnp.int32, scores.shape, 0)
    return jnp.where(row < live * TILE, scores, FLOOR)


def far_kernel(
    plan_ref, far_ref, came_ref, top_ref, total_ref, acc_ref, upt_ref, qs_ref,
    keep_ref, send_ref, ot_ref, lse_ref, delta_ref,
    kv_s, vt_s, s_buf, w_buf, dk_s, dv_s,
):
    dk_s[...] = jnp.zeros_like(dk_s)
    dv_s[...] = jnp.zeros_like(dv_s)
    kv_s[core()] = far_ref[...]
    kv_s[1 - core()] = came_ref[...]

    @pl.loop(0, BT)
    def _(t):
        for j in range(3):
            vt_s[t * 6 + j] = joined(halves(kv_s, 1, [t * 6 + j]), 0).T

    def work(r, width):
        count, tiles = listed_tiles(plan_ref, r, width)
        parts = parts_of(width)
        query = qs_ref[r]
        upstream = upt_ref[r]
        near_top = top_ref[r][:1]
        tops = top_ref[r]
        for lo, hi in parts:
            scores = dot_nt(joined(halves(kv_s, 0, tiles[lo:hi]), 0), query) * SCORE_SCALE
            if hi > width - STEP + 1:
                scores = only(scores, count - lo)
            s_buf[lo * TILE : hi * TILE] = scores
            tops = jnp.maximum(tops, fold(scores, jnp.max))
        top = jnp.max(tops, axis=0, keepdims=True)
        shrink = jnp.exp2(near_top - top)
        total = total_ref[r] * shrink
        acc = acc_ref[r] * shrink
        for lo, hi in parts:
            weights = jnp.exp2(s_buf[lo * TILE : hi * TILE] - top)
            total = total + fold(weights, jnp.sum)
            w_buf[lo * TILE : hi * TILE] = weights.astype(jnp.bfloat16)
        if width:
            acc = acc + dot(joined([vt_s[t] for t in tiles], 1), w_buf[: width * TILE])
        total = jnp.sum(total, axis=0, keepdims=True)
        attended = (acc * (1.0 / total)).astype(jnp.bfloat16)
        ot_ref[r] = attended
        delta = attended.astype(jnp.float32) * upstream.astype(jnp.float32)
        delta = jnp.sum(fold(delta, jnp.sum), axis=0, keepdims=True)
        lse = top + jnp.log2(total)
        lse_ref[r] = spread(lse)
        delta_ref[r] = spread(delta)
        for lo, hi in parts:
            probs = jnp.exp2(s_buf[lo * TILE : hi * TILE] - lse)
            grad_probs = dot(joined(halves(kv_s, 1, tiles[lo:hi]), 0), upstream)
            grad_scores = (probs * (grad_probs - delta)).astype(jnp.bfloat16)
            grad_value = dot_nt(probs.astype(jnp.bfloat16), upstream)
            grad_key = dot(grad_scores, query)
            for u, t in enumerate(tiles[lo:hi]):
                for half in range(2):
                    part = slice(u * TILE + half * HALF, u * TILE + (half + 1) * HALF)
                    dv_s[t + 3 * half] += grad_value[part]
                    dk_s[t + 3 * half] += grad_key[part]

    dk_s[...] = jnp.zeros_like(dk_s)
    dv_s[...] = jnp.zeros_like(dv_s)

    @pl.loop(0, BT)
    def _(r):
        by_width(plan_ref, r, functools.partial(work, r), 0)

    grad_key = (dk_s[...] * INV_ROOT).astype(jnp.bfloat16)
    grad_value = dv_s[...].astype(jnp.bfloat16)
    keep_ref[...] = jnp.where(core() == 0, grad_key, grad_value)
    send_ref[...] = jnp.where(core() == 0, grad_value, grad_key)


def score_gradients(scores, value, upstream, lse, delta):
    probs = jnp.exp2(scores - lse)
    grad_probs = dot_nt(value, upstream)
    return probs, (probs * (grad_probs - delta)).astype(jnp.bfloat16)


def listed_tiles(plan_ref, r, width):
    count = plan_ref[r, FAR_COUNT]
    listed = [plan_ref[r, FAR_LIST + u] for u in range(width)]
    sure = width - STEP
    return count, [t if u <= sure else jnp.where(u < count, t, 0) for u, t in enumerate(listed)]


def parts_of(width):
    return [(lo, min(lo + SUB, width)) for lo in range(0, width, SUB)]


def by_width(plan_ref, r, work, least):
    steps = lax.div(plan_ref[r, FAR_COUNT] + STEP - 1, STEP)
    for width in range(least, FAR + 1, STEP):
        pl.when(steps == width // STEP)(functools.partial(work, width))


def far_queries(plan_ref, kv_s, fkt_s, dq_s, r, query, upstream, lse, delta):
    def work(width):
        count, tiles = listed_tiles(plan_ref, r, width)
        for lo, hi in parts_of(width):
            scores = dot_nt(joined(halves(kv_s, 0, tiles[lo:hi]), 0), query) * SCORE_SCALE
            if hi > width - STEP + 1:
                scores = only(scores, count - lo)
            value = joined(halves(kv_s, 1, tiles[lo:hi]), 0)
            _, grad_scores = score_gradients(scores, value, upstream, lse, delta)
            dq_s[...] += dot(joined([fkt_s[t] for t in tiles[lo:hi]], 1), grad_scores)

    by_width(plan_ref, r, work, STEP)


def turned(dq_s):
    dq = dq_s[...] * INV_ROOT
    return joined([dq[:, :TILE].T, dq[:, TILE:].T], 1).astype(jnp.bfloat16)


def rest_kernel(
    plan_ref, rows_ref, other_ref, far_ref, came_ref, ot_ref, lse_ref, delta_ref,
    out_ref, keep_ref, send_ref, part_ref,
    own_s, kv_s, kt_s, fkt_s, dk_s, dv_s, dq_s,
):
    dk_s[...] = jnp.zeros_like(dk_s)
    dv_s[...] = jnp.zeros_like(dv_s)
    kv_s[core()] = far_ref[...]
    kv_s[1 - core()] = came_ref[...]

    @pl.loop(0, BT)
    def _(t):
        own_s[core(), t] = rows_ref[t, :, 512:640]
        own_s[1 - core(), t] = other_ref[t]
        kt_s[t] = own_s[0, t].T
        for j in range(3):
            fkt_s[t * 6 + j] = joined(halves(kv_s, 0, [t * 6 + j]), 0).T

    @pl.loop(0, BT)
    def _(r):
        query = stacked(rows_ref, r, 0)
        upstream = stacked(rows_ref, r, 256)
        lse = lse_ref[r][:1]
        delta = delta_ref[r][:1]
        attended = ot_ref[r].astype(jnp.float32)
        out_ref[r, :, 0:HD] = attended[:, :TILE].T.astype(jnp.bfloat16)
        out_ref[r, :, HD : 2 * HD] = attended[:, TILE:].T.astype(jnp.bfloat16)

        def own(width):
            count, tiles = own_tiles(plan_ref, r, width)
            dq = None
            for lo, hi in parts_of(width):
                part = tiles[lo:hi]
                scores = dot_nt(joined([own_s[0, t] for t in part], 0), query) * SCORE_SCALE
                scores = jnp.where(own_seen(count, lo, hi), scores, FLOOR)
                probs, grad_scores = score_gradients(
                    scores, joined([own_s[1, t] for t in part], 0), upstream, lse, delta
                )
                grad_value = dot(probs.astype(jnp.bfloat16), upstream)
                grad_key = dot(grad_scores, query)
                for u, t in enumerate(part):
                    dv_s[t] += grad_value[u * TILE : (u + 1) * TILE]
                    dk_s[t] += grad_key[u * TILE : (u + 1) * TILE]
                term = dot(joined([kt_s[t] for t in part], 1), grad_scores)
                dq = term if dq is None else dq + term
            dq_s[...] = dq

        pairs = lax.shift_right_logical(plan_ref[r, OWN_COUNT] + 2, 1)
        for width in range(2, BT + 1, 2):
            pl.when(pairs == width // 2)(functools.partial(own, width))

        @pl.when(r < EARLY)
        def _():
            far_queries(plan_ref, kv_s, fkt_s, dq_s, r, query, upstream, lse, delta)
            out_ref[r, :, 256:512] = turned(dq_s)

        @pl.when(r >= EARLY)
        def _():
            part_ref[r - EARLY] = dq_s[...]

    grad_key = dk_s[...] * INV_ROOT
    grad_value = dv_s[...]
    keep_ref[...] = jnp.where(core() == 0, grad_key, grad_value)
    send_ref[...] = jnp.where(core() == 0, grad_value, grad_key).astype(jnp.bfloat16)


def late_kernel(
    plan_ref, rows_ref, far_ref, came_ref, lse_ref, delta_ref, part_ref, late_ref, kv_s, fkt_s, dq_s
):
    kv_s[core()] = far_ref[...]
    kv_s[1 - core()] = came_ref[...]

    @pl.loop(0, BT)
    def _(t):
        for j in range(3):
            fkt_s[t * 6 + j] = joined(halves(kv_s, 0, [t * 6 + j]), 0).T

    @pl.loop(EARLY, BT)
    def _(r):
        query = stacked(rows_ref, r, 0)
        upstream = stacked(rows_ref, r, 256)
        dq_s[...] = part_ref[r - EARLY]
        far_queries(
            plan_ref, kv_s, fkt_s, dq_s, r, query, upstream, lse_ref[r][:1], delta_ref[r][:1]
        )
        late_ref[r - EARLY] = turned(dq_s)


VMEM = pl.BlockSpec(memory_space=pltpu.VMEM)
SMEM = pl.BlockSpec(memory_space=pltpu.SMEM)
ANY = pl.BlockSpec(memory_space=pl.ANY)
HBM = pl.BlockSpec(memory_space=pltpu.HBM)
BF16, F32 = jnp.bfloat16, jnp.float32


def shape(dims, dtype):
    return jax.ShapeDtypeStruct(dims, dtype)


def limit(mib):
    return pltpu.CompilerParams(vmem_limit_bytes=mib * 1024 * 1024)


def cost(us):
    return pl.CostEstimate(flops=us * 1_000_000_000, bytes_accessed=us * 100_000, transcendentals=0)


def pack(queries, upstream, keys, values):
    return pl.pallas_call(
        pack_kernel,
        out_shape=(shape((4, TILE, 640), BF16),) * 2,
        in_specs=[ANY] * 4,
        out_specs=(VMEM, VMEM),
        scratch_shapes=[
            pltpu.VMEM((TILE, 2048), BF16),
            pltpu.VMEM((TILE, 2048), BF16),
            pltpu.VMEM((TILE, 512), BF16),
            pltpu.VMEM((TILE, 512), BF16),
            pltpu.SemaphoreType.DMA((4,)),
        ],
        compiler_params=limit(60),
    )(queries, upstream, keys, values)


def simple(kernel, out_shape, *arrays):
    return pl.pallas_call(
        kernel,
        out_shape=out_shape,
        in_specs=[VMEM] * len(arrays),
        out_specs=jax.tree.map(lambda _: VMEM, out_shape),
        compiler_params=limit(16),
    )(*arrays)


def add_home(out, late, keep, came, home):
    return pl.pallas_call(
        add_kernel,
        out_shape=shape((BT, TILE, 640), BF16),
        in_specs=[VMEM] * 5,
        out_specs=VMEM,
        input_output_aliases={0: 0},
        compiler_params=limit(16),
    )(out, late, keep, came, home)


def near(order, mask, rows, other):
    return pl.pallas_call(
        near_kernel,
        out_shape=(
            shape((BT, PLAN), jnp.int32),
            shape((BT, 8, WIDE), F32),
            shape((BT, 8, WIDE), F32),
            shape((BT, HD, WIDE), F32),
            shape((BT, HD, WIDE), BF16),
            shape((BT, WIDE, HD), BF16),
        ),
        in_specs=[SMEM, ANY, VMEM, VMEM],
        out_specs=(SMEM, VMEM, VMEM, VMEM, VMEM, VMEM),
        scratch_shapes=[
            pltpu.VMEM((2, BT, TILE, HD), BF16),
            pltpu.VMEM((BT, HD, TILE), BF16),
            pltpu.SMEM((BT, 128), jnp.int32),
            pltpu.SemaphoreType.DMA,
        ],
        compiler_params=limit(60),
        cost_estimate=cost(12),
    )(order, mask, rows, other)


def far_part(plan, far, came, top, total, acc, upt, qs):
    return pl.pallas_call(
        far_kernel,
        out_shape=(
            shape((2 * FAR, HALF, HD), BF16),
            shape((2 * FAR, HALF, HD), BF16),
            shape((BT, HD, WIDE), BF16),
            shape((BT, 8, WIDE), F32),
            shape((BT, 8, WIDE), F32),
        ),
        in_specs=[SMEM] + [VMEM] * 7,
        out_specs=(VMEM,) * 5,
        scratch_shapes=[
            pltpu.VMEM((2, 2 * FAR, HALF, HD), BF16),
            pltpu.VMEM((2 * FAR, HD, TILE), BF16),
            pltpu.VMEM((FAR * TILE, WIDE), F32),
            pltpu.VMEM((FAR * TILE, WIDE), BF16),
            pltpu.VMEM((2 * FAR, HALF, HD), F32),
            pltpu.VMEM((2 * FAR, HALF, HD), F32),
        ],
        compiler_params=limit(60),
        cost_estimate=cost(25),
    )(plan, far, came, top, total, acc, upt, qs)


def rest_part(plan, rows, other, far, came, ot, lse, delta):
    return pl.pallas_call(
        rest_kernel,
        out_shape=(
            shape((BT, TILE, 640), BF16),
            shape((BT, TILE, HD), F32),
            shape((BT, TILE, HD), BF16),
            shape((BT - EARLY, HD, WIDE), F32),
        ),
        in_specs=[SMEM] + [VMEM] * 7,
        out_specs=(VMEM,) * 4,
        scratch_shapes=[
            pltpu.VMEM((2, BT, TILE, HD), BF16),
            pltpu.VMEM((2, 2 * FAR, HALF, HD), BF16),
            pltpu.VMEM((BT, HD, TILE), BF16),
            pltpu.VMEM((2 * FAR, HD, TILE), BF16),
            pltpu.VMEM((BT, TILE, HD), F32),
            pltpu.VMEM((BT, TILE, HD), F32),
            pltpu.VMEM((HD, WIDE), F32),
        ],
        compiler_params=limit(60),
        cost_estimate=cost(18),
    )(plan, rows, other, far, came, ot, lse, delta)


def late_part(plan, rows, far, came, lse, delta, part):
    return pl.pallas_call(
        late_kernel,
        out_shape=shape((BT - EARLY, TILE, WIDE), BF16),
        in_specs=[SMEM] + [VMEM] * 6,
        out_specs=VMEM,
        scratch_shapes=[
            pltpu.VMEM((2, 2 * FAR, HALF, HD), BF16),
            pltpu.VMEM((2 * FAR, HD, TILE), BF16),
            pltpu.VMEM((HD, WIDE), F32),
        ],
        compiler_params=limit(60),
        cost_estimate=cost(10),
    )(plan, rows, far, came, lse, delta, part)


def routed(kernel, order, array, out_shape):
    return pl.pallas_call(
        kernel,
        out_shape=shape(out_shape, BF16),
        in_specs=[SMEM, VMEM],
        out_specs=VMEM,
        scratch_shapes=[pltpu.SMEM((NB,), jnp.int32)],
        compiler_params=limit(16),
    )(order, array)


def over_heads(array):
    return lax.all_to_all(array, "head", split_axis=0, concat_axis=0, tiled=True)


SERVING = [
    [(2 * chip + u) * 8 + beta * 4 + g for chip in range(8) for beta in range(2)]
    for u in range(2)
    for g in range(4)
]


def over_blocks(array):
    return lax.all_to_all(
        array, ("blk", "head"), split_axis=0, concat_axis=0, axis_index_groups=SERVING, tiled=True
    )


def to_other_core(array):
    return lax.ppermute(array, "blk", [(i, i ^ 1) for i in range(16)])


def on_device(queries, keys, values, upstream, tile_mask, tile_order):
    order = tile_order[0]
    keep, send = pack(queries[0], upstream[0], keys[0], values[0])
    both = simple(merge_kernel, shape((8, TILE, 640), BF16), keep, to_other_core(send))
    rows = over_heads(both)
    own = rows[:, :, 512:]
    other = to_other_core(own)
    pieces = over_blocks(own.reshape(NB, HALF, HD))
    chosen = routed(gather_kernel, order, pieces, (NB, 3, HALF, HD))
    far = over_blocks(chosen).reshape(2 * FAR, HALF, HD)
    begun = near(order, tile_mask[0], rows, other)
    far, *begun = lax.optimization_barrier((far, *begun))
    plan = begun[0]
    came = to_other_core(far)
    keep, send, ot, lse, delta = far_part(plan, far, came, *begun[1:])
    dfar = (keep.astype(F32) + to_other_core(send).astype(F32)).astype(BF16)
    parts = over_blocks(dfar.reshape(NB, 3, HALF, HD))
    out, keep, send, part = rest_part(plan, rows, other, far, came, ot, lse, delta)
    parts, out, keep, send, part = lax.optimization_barrier((parts, out, keep, send, part))
    summed = routed(sum_kernel, order, parts, (NB, HALF, HD))
    summed, part = lax.optimization_barrier((summed, part))
    home = over_blocks(summed).reshape(BT, TILE, HD)
    late = late_part(plan, rows, far, came, lse, delta, part)
    back = over_heads(add_home(out, late, keep, to_other_core(send), home))
    came = to_other_core(simple(pick_kernel, shape((4, TILE, 640), BF16), back))
    wide, slim = shape((TILE, 2048), BF16), shape((TILE, 512), BF16)
    outs = simple(unpack_kernel, (wide, wide, slim, slim), back, came)
    return tuple(array[None] for array in outs)


def solution(mesh):
    split = P(None, ("blk", "head"), None)
    return jax.shard_map(
        on_device,
        mesh=mesh,
        in_specs=(split, split, split, split, P(), P()),
        out_specs=(split, split, split, split),
        check_vma=False,
    )
```

```python
import functools
import math

import jax
import jax.numpy as jnp
from jax import lax
from jax.experimental import pallas as pl
from jax.experimental.pallas import tpu as pltpu
from jax.sharding import PartitionSpec as P

HD = 128
TILE = 128
WIDE = 256
BT = 8
NB = 16
FAR = 24
HALF = 64
EARLY = 5
SUB = 4
STEP = 4
INV_ROOT = 1.0 / math.sqrt(HD)
SCORE_SCALE = INV_ROOT * math.log2(math.e)
FLOOR = -1e30

OWN_COUNT, FAR_COUNT, OWN_LIST, FAR_LIST, PLAN = 0, 1, 8, 16, 64

NT = (((1,), (1,)), ((), ()))


def dot(a, b):
    return jnp.dot(a, b, preferred_element_type=jnp.float32)


def dot_nt(a, b):
    return lax.dot_general(a, b, NT, preferred_element_type=jnp.float32)


def block_of(order_ref, index):
    return lax.shift_right_logical(order_ref[index * BT], 3)


def invert_blocks(order_ref, where_ref):
    for k in range(NB):
        where_ref[block_of(order_ref, k)] = k


def core():
    return lax.axis_index("blk") & 1


def served_block():
    return (lax.axis_index("blk") & ~1) + lax.shift_right_logical(lax.axis_index("head"), 2)


def pair_columns(group, which):
    return pl.ds(pl.multiple_of((2 * group + which) * WIDE, WIDE), WIDE)


def pack_kernel(*refs):
    sources, (keep_ref, send_ref), landed, sems = refs[:4], refs[4:6], refs[6:10], refs[10]
    copies = [
        pltpu.make_async_copy(source, target, sems.at[n])
        for n, (source, target) in enumerate(zip(sources, landed))
    ]
    for copy in copies:
        copy.start()
    for copy in copies:
        copy.wait()
    q_ref, d_ref, k_ref, v_ref = landed
    me = core()
    for g in range(4):
        for ref, which in ((keep_ref, me), (send_ref, 1 - me)):
            ref[g, :, 0:256] = q_ref[:, pair_columns(g, which)]
            ref[g, :, 256:512] = d_ref[:, pair_columns(g, which)]
        key = k_ref[:, g * HD : (g + 1) * HD]
        value = v_ref[:, g * HD : (g + 1) * HD]
        keep_ref[g, :, 512:640] = jnp.where(me == 0, key, value)
        send_ref[g, :, 512:640] = jnp.where(me == 0, value, key)


def merge_kernel(keep_ref, came_ref, out_ref):
    me = core()
    for g in range(4):
        out_ref[me * 4 + g] = keep_ref[g]
        out_ref[(1 - me) * 4 + g] = came_ref[g]


def pick_kernel(back_ref, send_ref):
    for g in range(4):
        send_ref[g] = back_ref[(1 - core()) * 4 + g]


def unpack_kernel(back_ref, came_ref, o_ref, dq_ref, dk_ref, dv_ref):
    me = core()
    for g in range(4):
        mine = back_ref[me * 4 + g]
        for piece, which in ((mine, me), (came_ref[g], 1 - me)):
            o_ref[:, pair_columns(g, which)] = piece[:, 0:256]
            dq_ref[:, pair_columns(g, which)] = piece[:, 256:512]
        a, b = mine[:, 512:640], came_ref[g, :, 512:640]
        dk_ref[:, g * HD : (g + 1) * HD] = jnp.where(me == 0, a, b)
        dv_ref[:, g * HD : (g + 1) * HD] = jnp.where(me == 0, b, a)


def add_kernel(rows_ref, late_ref, keep_ref, came_ref, home_ref, out_ref):
    out_ref[EARLY:, :, 256:512] = late_ref[...]
    total = keep_ref[...] + came_ref[...].astype(jnp.float32) + home_ref[...].astype(jnp.float32)
    out_ref[:, :, 512:640] = total.astype(jnp.bfloat16)


def gather_kernel(order_ref, pieces_ref, out_ref, where_ref):
    invert_blocks(order_ref, where_ref)

    @pl.loop(0, NB)
    def _(k):
        b = block_of(order_ref, k)
        for j in range(3):
            src = jnp.maximum(b - 1 - j, 0) if j < 2 else 0
            out_ref[k, j] = pieces_ref[where_ref[src]]


def sum_kernel(order_ref, parts_ref, out_ref, where_ref):
    invert_blocks(order_ref, where_ref)

    @pl.loop(0, NB)
    def _(k):
        b = block_of(order_ref, k)
        near = parts_ref[where_ref[jnp.minimum(b + 1, NB - 1)], 0].astype(jnp.float32)
        far = parts_ref[where_ref[jnp.minimum(b + 2, NB - 1)], 1].astype(jnp.float32)
        total = jnp.where(b + 1 < NB, near, 0.0) + jnp.where(b + 2 < NB, far, 0.0)
        out_ref[k] = total.astype(jnp.bfloat16)

    total = parts_ref[where_ref[1], 0].astype(jnp.float32)
    total = total + parts_ref[where_ref[2], 1].astype(jnp.float32)
    for b in range(3, NB):
        total = total + parts_ref[where_ref[b], 2].astype(jnp.float32)
    out_ref[where_ref[0]] = total.astype(jnp.bfloat16)


def fold(x, op):
    return op(x.reshape(-1, 8, WIDE), axis=0)


def spread(x):
    return jnp.broadcast_to(x, (8, WIDE))


def joined(refs, axis):
    return jnp.concatenate(refs, axis=axis)


def stacked(rows_ref, r, lo):
    return joined([rows_ref[r, :, lo : lo + HD], rows_ref[r, :, lo + HD : lo + 2 * HD]], 0)


def own_seen(count, lo, hi):
    k_pos = lax.broadcasted_iota(jnp.int32, ((hi - lo) * TILE, WIDE), 0) + lo * TILE
    q_pos = lax.broadcasted_iota(jnp.int32, ((hi - lo) * TILE, WIDE), 1) % TILE
    limit = jnp.where(k_pos < TILE, q_pos + 1, (count + 1) * TILE)
    return k_pos < limit


def own_tiles(plan_ref, r, width):
    count = plan_ref[r, OWN_COUNT]
    rest = [jnp.where(u < count, plan_ref[r, OWN_LIST + u], r) for u in range(width - 1)]
    return count, [r] + rest


def near_kernel(
    order_ref, mask_ref, rows_ref, came_ref, plan_ref, top_ref, total_ref, acc_ref, upt_ref, qs_ref,
    own_s, vt_s, mask_s, sem,
):
    b = block_of(order_ref, served_block())
    copy = pltpu.make_async_copy(mask_ref.at[pl.ds(pl.multiple_of(b * BT, BT), BT)], mask_s, sem)
    copy.start()

    @pl.loop(0, BT)
    def _(t):
        own_s[core(), t] = rows_ref[t, :, 512:640]
        own_s[1 - core(), t] = came_ref[t]
        vt_s[t] = own_s[1, t].T

    copy.wait()

    @pl.loop(0, BT)
    def _(r):
        own = jnp.int32(0)
        for t in range(BT - 1):
            plan_ref[r, OWN_LIST + own] = t
            own = own + ((mask_s[r, b * BT + t] == 1) & (t < r)).astype(jnp.int32)
        plan_ref[r, OWN_COUNT] = own
        far = jnp.int32(0)
        for t in range(BT):
            for j in range(3):
                column = jnp.maximum(b - 1 - j, 0) * BT + t if j < 2 else t
                plan_ref[r, FAR_LIST + far] = t * 6 + j
                far = far + ((mask_s[r, column] == 1) & (b > j)).astype(jnp.int32)
        plan_ref[r, FAR_COUNT] = far

    @pl.loop(0, BT)
    def _(r):
        query = stacked(rows_ref, r, 0)
        qs_ref[r] = query

        def own(width):
            count, tiles = own_tiles(plan_ref, r, width)
            scores = dot_nt(joined([own_s[0, t] for t in tiles], 0), query) * SCORE_SCALE
            scores = jnp.where(own_seen(count, 0, width), scores, FLOOR)
            top = jnp.max(fold(scores, jnp.max), axis=0, keepdims=True)
            weights = jnp.exp2(scores - top)
            top_ref[r] = spread(top)
            total_ref[r] = fold(weights, jnp.sum)
            acc_ref[r] = dot(joined([vt_s[t] for t in tiles], 1), weights.astype(jnp.bfloat16))

        pairs = lax.shift_right_logical(plan_ref[r, OWN_COUNT] + 2, 1)
        for width in range(2, BT + 1, 2):
            pl.when(pairs == width // 2)(functools.partial(own, width))

        upt_ref[r] = joined([rows_ref[r, :, 256:384].T, rows_ref[r, :, 384:512].T], 1)


def halves(ref, part, tiles):
    return [ref[part, t + 3 * half] for t in tiles for half in range(2)]


def only(scores, live):
    row = lax.broadcasted_iota(jnp.int32, scores.shape, 0)
    return jnp.where(row < live * TILE, scores, FLOOR)


def far_kernel(
    plan_ref, far_ref, came_ref, top_ref, total_ref, acc_ref, upt_ref, qs_ref,
    keep_ref, send_ref, ot_ref, lse_ref, delta_ref,
    kv_s, vt_s, s_buf, w_buf, dk_s, dv_s,
):
    dk_s[...] = jnp.zeros_like(dk_s)
    dv_s[...] = jnp.zeros_like(dv_s)
    kv_s[core()] = far_ref[...]
    kv_s[1 - core()] = came_ref[...]

    @pl.loop(0, BT)
    def _(t):
        for j in range(3):
            vt_s[t * 6 + j] = joined(halves(kv_s, 1, [t * 6 + j]), 0).T

    def work(r, width):
        count, tiles = listed_tiles(plan_ref, r, width)
        parts = parts_of(width)
        query = qs_ref[r]
        upstream = upt_ref[r]
        near_top = top_ref[r][:1]
        tops = top_ref[r]
        for lo, hi in parts:
            scores = dot_nt(joined(halves(kv_s, 0, tiles[lo:hi]), 0), query) * SCORE_SCALE
            if hi > width - STEP + 1:
                scores = only(scores, count - lo)
            s_buf[lo * TILE : hi * TILE] = scores
            tops = jnp.maximum(tops, fold(scores, jnp.max))
        top = jnp.max(tops, axis=0, keepdims=True)
        shrink = jnp.exp2(near_top - top)
        total = total_ref[r] * shrink
        acc = acc_ref[r] * shrink
        for lo, hi in parts:
            weights = jnp.exp2(s_buf[lo * TILE : hi * TILE] - top)
            total = total + fold(weights, jnp.sum)
            w_buf[lo * TILE : hi * TILE] = weights.astype(jnp.bfloat16)
        if width:
            acc = acc + dot(joined([vt_s[t] for t in tiles], 1), w_buf[: width * TILE])
        total = jnp.sum(total, axis=0, keepdims=True)
        attended = (acc * (1.0 / total)).astype(jnp.bfloat16)
        ot_ref[r] = attended
        delta = attended.astype(jnp.float32) * upstream.astype(jnp.float32)
        delta = jnp.sum(fold(delta, jnp.sum), axis=0, keepdims=True)
        lse = top + jnp.log2(total)
        lse_ref[r] = spread(lse)
        delta_ref[r] = spread(delta)
        for lo, hi in parts:
            probs = jnp.exp2(s_buf[lo * TILE : hi * TILE] - lse)
            grad_probs = dot(joined(halves(kv_s, 1, tiles[lo:hi]), 0), upstream)
            grad_scores = (probs * (grad_probs - delta)).astype(jnp.bfloat16)
            grad_value = dot_nt(probs.astype(jnp.bfloat16), upstream)
            grad_key = dot(grad_scores, query)
            for u, t in enumerate(tiles[lo:hi]):
                for half in range(2):
                    part = slice(u * TILE + half * HALF, u * TILE + (half + 1) * HALF)
                    dv_s[t + 3 * half] += grad_value[part]
                    dk_s[t + 3 * half] += grad_key[part]

    dk_s[...] = jnp.zeros_like(dk_s)
    dv_s[...] = jnp.zeros_like(dv_s)

    @pl.loop(0, BT)
    def _(r):
        by_width(plan_ref, r, functools.partial(work, r), 0)

    def cast(key_ref, value_ref):
        key_ref[...] = (dk_s[...] * INV_ROOT).astype(jnp.bfloat16)
        value_ref[...] = dv_s[...].astype(jnp.bfloat16)

    pl.when(core() == 0)(lambda: cast(keep_ref, send_ref))
    pl.when(core() == 1)(lambda: cast(send_ref, keep_ref))


def score_gradients(scores, value, upstream, lse, delta):
    probs = jnp.exp2(scores - lse)
    grad_probs = dot(value, upstream)
    return probs, (probs * (grad_probs - delta)).astype(jnp.bfloat16)


def listed_tiles(plan_ref, r, width):
    count = plan_ref[r, FAR_COUNT]
    listed = [plan_ref[r, FAR_LIST + u] for u in range(width)]
    sure = width - STEP
    return count, [t if u <= sure else jnp.where(u < count, t, 0) for u, t in enumerate(listed)]


def parts_of(width):
    return [(lo, min(lo + SUB, width)) for lo in range(0, width, SUB)]


def by_width(plan_ref, r, work, least):
    steps = lax.div(plan_ref[r, FAR_COUNT] + STEP - 1, STEP)
    for width in range(least, FAR + 1, STEP):
        pl.when(steps == width // STEP)(functools.partial(work, width))


def far_queries(plan_ref, kv_s, fkt_s, dq_s, r, query, upstream, lse, delta):
    def work(width):
        count, tiles = listed_tiles(plan_ref, r, width)
        for lo, hi in parts_of(width):
            scores = dot_nt(joined(halves(kv_s, 0, tiles[lo:hi]), 0), query) * SCORE_SCALE
            if hi > width - STEP + 1:
                scores = only(scores, count - lo)
            value = joined(halves(kv_s, 1, tiles[lo:hi]), 0)
            _, grad_scores = score_gradients(scores, value, upstream, lse, delta)
            dq_s[...] += dot(joined([fkt_s[t] for t in tiles[lo:hi]], 1), grad_scores)

    by_width(plan_ref, r, work, STEP)


def turned(dq_s):
    dq = dq_s[...] * INV_ROOT
    return joined([dq[:, :TILE].T, dq[:, TILE:].T], 1).astype(jnp.bfloat16)


def rest_kernel(
    plan_ref, qs_ref, upt_ref, own_ref, other_ref, far_ref, came_ref, ot_ref, lse_ref, delta_ref,
    out_ref, keep_ref, send_ref, part_ref,
    own_s, kv_s, kt_s, fkt_s, dk_s, dv_s, dq_s,
):
    dk_s[...] = jnp.zeros_like(dk_s)
    dv_s[...] = jnp.zeros_like(dv_s)
    kv_s[core()] = far_ref[...]
    kv_s[1 - core()] = came_ref[...]

    @pl.loop(0, BT)
    def _(t):
        own_s[core(), t] = own_ref[t]
        own_s[1 - core(), t] = other_ref[t]
        kt_s[t] = own_s[0, t].T
        for j in range(3):
            fkt_s[t * 6 + j] = joined(halves(kv_s, 0, [t * 6 + j]), 0).T

    @pl.loop(0, BT)
    def _(r):
        query = qs_ref[r]
        upstream = upt_ref[r]
        lse = lse_ref[r][:1]
        delta = delta_ref[r][:1]
        attended = ot_ref[r].astype(jnp.float32)
        out_ref[r, :, 0:HD] = attended[:, :TILE].T.astype(jnp.bfloat16)
        out_ref[r, :, HD : 2 * HD] = attended[:, TILE:].T.astype(jnp.bfloat16)

        def own(width):
            count, tiles = own_tiles(plan_ref, r, width)
            dq = None
            for lo, hi in parts_of(width):
                part = tiles[lo:hi]
                scores = dot_nt(joined([own_s[0, t] for t in part], 0), query) * SCORE_SCALE
                scores = jnp.where(own_seen(count, lo, hi), scores, FLOOR)
                probs, grad_scores = score_gradients(
                    scores, joined([own_s[1, t] for t in part], 0), upstream, lse, delta
                )
                grad_value = dot_nt(probs.astype(jnp.bfloat16), upstream)
                grad_key = dot(grad_scores, query)
                for u, t in enumerate(part):
                    dv_s[t] += grad_value[u * TILE : (u + 1) * TILE]
                    dk_s[t] += grad_key[u * TILE : (u + 1) * TILE]
                term = dot(joined([kt_s[t] for t in part], 1), grad_scores)
                dq = term if dq is None else dq + term
            dq_s[...] = dq

        pairs = lax.shift_right_logical(plan_ref[r, OWN_COUNT] + 2, 1)
        for width in range(2, BT + 1, 2):
            pl.when(pairs == width // 2)(functools.partial(own, width))

        @pl.when(r < EARLY)
        def _():
            far_queries(plan_ref, kv_s, fkt_s, dq_s, r, query, upstream, lse, delta)
            out_ref[r, :, 256:512] = turned(dq_s)

        @pl.when(r >= EARLY)
        def _():
            part_ref[r - EARLY] = dq_s[...]

    grad_key = dk_s[...] * INV_ROOT
    grad_value = dv_s[...]
    keep_ref[...] = jnp.where(core() == 0, grad_key, grad_value)
    send_ref[...] = jnp.where(core() == 0, grad_value, grad_key).astype(jnp.bfloat16)


def late_kernel(
    plan_ref, qs_ref, upt_ref, far_ref, came_ref, lse_ref, delta_ref, part_ref, late_ref, kv_s, fkt_s, dq_s
):
    kv_s[core()] = far_ref[...]
    kv_s[1 - core()] = came_ref[...]

    @pl.loop(0, BT)
    def _(t):
        for j in range(3):
            fkt_s[t * 6 + j] = joined(halves(kv_s, 0, [t * 6 + j]), 0).T

    @pl.loop(EARLY, BT)
    def _(r):
        query = qs_ref[r]
        upstream = upt_ref[r]
        dq_s[...] = part_ref[r - EARLY]
        far_queries(
            plan_ref, kv_s, fkt_s, dq_s, r, query, upstream, lse_ref[r][:1], delta_ref[r][:1]
        )
        late_ref[r - EARLY] = turned(dq_s)


VMEM = pl.BlockSpec(memory_space=pltpu.VMEM)
SMEM = pl.BlockSpec(memory_space=pltpu.SMEM)
ANY = pl.BlockSpec(memory_space=pl.ANY)
HBM = pl.BlockSpec(memory_space=pltpu.HBM)
BF16, F32 = jnp.bfloat16, jnp.float32


def shape(dims, dtype):
    return jax.ShapeDtypeStruct(dims, dtype)


def limit(mib):
    return pltpu.CompilerParams(vmem_limit_bytes=mib * 1024 * 1024)


def cost(us):
    return pl.CostEstimate(flops=us * 1_000_000_000, bytes_accessed=us * 100_000, transcendentals=0)


def pack(queries, upstream, keys, values):
    return pl.pallas_call(
        pack_kernel,
        out_shape=(shape((4, TILE, 640), BF16),) * 2,
        in_specs=[ANY] * 4,
        out_specs=(VMEM, VMEM),
        scratch_shapes=[
            pltpu.VMEM((TILE, 2048), BF16),
            pltpu.VMEM((TILE, 2048), BF16),
            pltpu.VMEM((TILE, 512), BF16),
            pltpu.VMEM((TILE, 512), BF16),
            pltpu.SemaphoreType.DMA((4,)),
        ],
        compiler_params=limit(60),
    )(queries, upstream, keys, values)


def simple(kernel, out_shape, *arrays):
    return pl.pallas_call(
        kernel,
        out_shape=out_shape,
        in_specs=[VMEM] * len(arrays),
        out_specs=jax.tree.map(lambda _: VMEM, out_shape),
        compiler_params=limit(16),
    )(*arrays)


def add_home(out, late, keep, came, home):
    return pl.pallas_call(
        add_kernel,
        out_shape=shape((BT, TILE, 640), BF16),
        in_specs=[VMEM] * 5,
        out_specs=VMEM,
        input_output_aliases={0: 0},
        compiler_params=limit(16),
    )(out, late, keep, came, home)


def near(order, mask, rows, other):
    return pl.pallas_call(
        near_kernel,
        out_shape=(
            shape((BT, PLAN), jnp.int32),
            shape((BT, 8, WIDE), F32),
            shape((BT, 8, WIDE), F32),
            shape((BT, HD, WIDE), F32),
            shape((BT, HD, WIDE), BF16),
            shape((BT, WIDE, HD), BF16),
        ),
        in_specs=[SMEM, ANY, VMEM, VMEM],
        out_specs=(SMEM, VMEM, VMEM, VMEM, VMEM, VMEM),
        scratch_shapes=[
            pltpu.VMEM((2, BT, TILE, HD), BF16),
            pltpu.VMEM((BT, HD, TILE), BF16),
            pltpu.SMEM((BT, 128), jnp.int32),
            pltpu.SemaphoreType.DMA,
        ],
        compiler_params=limit(60),
        cost_estimate=cost(12),
    )(order, mask, rows, other)


def far_part(plan, far, came, top, total, acc, upt, qs):
    return pl.pallas_call(
        far_kernel,
        out_shape=(
            shape((2 * FAR, HALF, HD), BF16),
            shape((2 * FAR, HALF, HD), BF16),
            shape((BT, HD, WIDE), BF16),
            shape((BT, 8, WIDE), F32),
            shape((BT, 8, WIDE), F32),
        ),
        in_specs=[SMEM] + [VMEM] * 7,
        out_specs=(VMEM,) * 5,
        scratch_shapes=[
            pltpu.VMEM((2, 2 * FAR, HALF, HD), BF16),
            pltpu.VMEM((2 * FAR, HD, TILE), BF16),
            pltpu.VMEM((FAR * TILE, WIDE), F32),
            pltpu.VMEM((FAR * TILE, WIDE), BF16),
            pltpu.VMEM((2 * FAR, HALF, HD), F32),
            pltpu.VMEM((2 * FAR, HALF, HD), F32),
        ],
        compiler_params=limit(60),
        cost_estimate=cost(25),
    )(plan, far, came, top, total, acc, upt, qs)


def rest_part(plan, qs, upt, own, other, far, came, ot, lse, delta):
    return pl.pallas_call(
        rest_kernel,
        out_shape=(
            shape((BT, TILE, 640), BF16),
            shape((BT, TILE, HD), F32),
            shape((BT, TILE, HD), BF16),
            shape((BT - EARLY, HD, WIDE), F32),
        ),
        in_specs=[SMEM] + [VMEM] * 9,
        out_specs=(VMEM,) * 4,
        scratch_shapes=[
            pltpu.VMEM((2, BT, TILE, HD), BF16),
            pltpu.VMEM((2, 2 * FAR, HALF, HD), BF16),
            pltpu.VMEM((BT, HD, TILE), BF16),
            pltpu.VMEM((2 * FAR, HD, TILE), BF16),
            pltpu.VMEM((BT, TILE, HD), F32),
            pltpu.VMEM((BT, TILE, HD), F32),
            pltpu.VMEM((HD, WIDE), F32),
        ],
        compiler_params=limit(60),
        cost_estimate=cost(18),
    )(plan, qs, upt, own, other, far, came, ot, lse, delta)


def late_part(plan, qs, upt, far, came, lse, delta, part):
    return pl.pallas_call(
        late_kernel,
        out_shape=shape((BT - EARLY, TILE, WIDE), BF16),
        in_specs=[SMEM] + [VMEM] * 7,
        out_specs=VMEM,
        scratch_shapes=[
            pltpu.VMEM((2, 2 * FAR, HALF, HD), BF16),
            pltpu.VMEM((2 * FAR, HD, TILE), BF16),
            pltpu.VMEM((HD, WIDE), F32),
        ],
        compiler_params=limit(60),
        cost_estimate=cost(10),
    )(plan, qs, upt, far, came, lse, delta, part)


def routed(kernel, order, array, out_shape):
    return pl.pallas_call(
        kernel,
        out_shape=shape(out_shape, BF16),
        in_specs=[SMEM, VMEM],
        out_specs=VMEM,
        scratch_shapes=[pltpu.SMEM((NB,), jnp.int32)],
        compiler_params=limit(16),
    )(order, array)


def over_heads(array):
    return lax.all_to_all(array, "head", split_axis=0, concat_axis=0, tiled=True)


SERVING = [
    [(2 * chip + u) * 8 + beta * 4 + g for chip in range(8) for beta in range(2)]
    for u in range(2)
    for g in range(4)
]


def over_blocks(array):
    return lax.all_to_all(
        array, ("blk", "head"), split_axis=0, concat_axis=0, axis_index_groups=SERVING, tiled=True
    )


def to_other_core(array):
    return lax.ppermute(array, "blk", [(i, i ^ 1) for i in range(16)])


def on_device(queries, keys, values, upstream, tile_mask, tile_order):
    order = tile_order[0]
    keep, send = pack(queries[0], upstream[0], keys[0], values[0])
    both = simple(merge_kernel, shape((8, TILE, 640), BF16), keep, to_other_core(send))
    rows = over_heads(both)
    own = rows[:, :, 512:]
    other = to_other_core(own)
    pieces = over_blocks(own.reshape(NB, HALF, HD))
    chosen = routed(gather_kernel, order, pieces, (NB, 3, HALF, HD))
    far = over_blocks(chosen).reshape(2 * FAR, HALF, HD)
    begun = near(order, tile_mask[0], rows, other)
    far, *begun = lax.optimization_barrier((far, *begun))
    plan, upt, qs = begun[0], begun[4], begun[5]
    came = to_other_core(far)
    keep, send, ot, lse, delta = far_part(plan, far, came, *begun[1:])
    dfar = (keep.astype(F32) + to_other_core(send).astype(F32)).astype(BF16)
    parts = over_blocks(dfar.reshape(NB, 3, HALF, HD))
    out, keep, send, part = rest_part(plan, qs, upt, own, other, far, came, ot, lse, delta)
    parts, out, keep, send, part = lax.optimization_barrier((parts, out, keep, send, part))
    summed = routed(sum_kernel, order, parts, (NB, HALF, HD))
    summed, part = lax.optimization_barrier((summed, part))
    home = over_blocks(summed).reshape(BT, TILE, HD)
    late = late_part(plan, qs, upt, far, came, lse, delta, part)
    back = over_heads(add_home(out, late, keep, to_other_core(send), home))
    came = to_other_core(simple(pick_kernel, shape((4, TILE, 640), BF16), back))
    wide, slim = shape((TILE, 2048), BF16), shape((TILE, 512), BF16)
    outs = simple(unpack_kernel, (wide, wide, slim, slim), back, came)
    return tuple(array[None] for array in outs)


def solution(mesh):
    split = P(None, ("blk", "head"), None)
    return jax.shard_map(
        on_device,
        mesh=mesh,
        in_specs=(split, split, split, split, P(), P()),
        out_specs=(split, split, split, split),
        check_vma=False,
    )
```
